32 devices in a mesh: rows: 8 (over z, y), vec: 4 (over x, core).
Axes of the slice: x: 2, y: 2, z: 4, core: 2. Of those that a mesh axis runs over, the one named last changes fastest.
Arguments:
- self_tiles: bfloat16 [64, 256, 256], P('rows'), may hold values from 0.01 to 1, as said below
- link_tiles: bfloat16 [64, 3, 256, 256], P('rows'), may hold values from 0.01 to 1, as said below
- links: int32 [64, 3], replicated, may hold values from 0 to 63, as said below
- coarse_row: int32 [64], replicated, may hold values from 0 to 31, as said below
- vectors: float32 [16, 16384], P('vec', 'rows'), may hold values from -70 to 70
- directions: float32 [16, 16384], P('vec', 'rows'), may hold values from -70 to 70
Outputs:
- residual: float32 [16, 16384], P('vec', 'rows')
- corrected: float32 [16, 16384], P('vec', 'rows')
- projected: float32 [48, 48], replicated
The draws below stay inside these ranges and needn't reach their ends.
Inputs may be any that keep to these rules, and one draw needn't show every extreme that they name: For each slot s, links[., s] pairs the row blocks: links[links[b, s], s] = b and links[b, s] != b; the linked block lies on the same slab of 8 blocks as b or on the slab just before or after it (blocks numbered slab by slab). `coarse_row`: each coarse row numbers exactly two row blocks. `self_tiles`: each tile is symmetric, entries positive. link_tiles[b, s] is the transpose of link_tiles[links[b, s], s]; entries positive.
All inputs are finite; a program needn't handle non-finite values.
Results may differ from the reference program's by a relative error of at most 0.0029.
Values may be sent and summed in bfloat16 or wider, within the bound.
A program may use at most 128 MiB of HBM per device.

```python
import math
import jax
import jax.numpy as jnp
from jax import lax

BS = 256
K = 16
LINKS = 3
RB_DEV = 8
NB = 64
NC = 32
ROWS = 16384
N_ROWS = 8


def pairing_order(window_key, first_block, length, windows):
    window_keys = jax.random.split(window_key, windows)
    shuffled = jax.vmap(lambda single_key: jax.random.permutation(single_key, length))(window_keys)
    offsets = first_block + jnp.arange(windows, dtype=jnp.int32) * length
    return (shuffled.astype(jnp.int32) + offsets[:, None]).reshape(-1)


def make_links(key):
    link_key = jax.random.fold_in(key, 11)
    columns = []
    for slot_index in range(LINKS):
        slot_key = jax.random.fold_in(link_key, slot_index)
        if slot_index % 2 == 0:
            ordering = pairing_order(slot_key, 0, 2 * RB_DEV, N_ROWS // 2)
        else:
            key_low, key_mid, key_high = jax.random.split(slot_key, 3)
            ordering = jnp.concatenate([pairing_order(key_low, 0, RB_DEV, 1), pairing_order(key_mid, RB_DEV, 2 * RB_DEV, N_ROWS // 2 - 1), pairing_order(key_high, NB - RB_DEV, RB_DEV, 1)])
        paired = ordering.reshape(-1, 2)
        partner = jnp.zeros((NB,), jnp.int32).at[paired[:, 0]].set(paired[:, 1]).at[paired[:, 1]].set(paired[:, 0])
        columns.append(partner)
    return jnp.stack(columns, axis=1).astype(jnp.int32)


def tile_values(tile_key, shape):
    return jnp.exp(jax.random.uniform(tile_key, shape, jnp.float32, math.log(0.01), 0.0))


def draw_links(key, part):
    return make_links(key)


def draw_coarse_row(key, part):
    ordering = jax.random.permutation(jax.random.fold_in(key, 41), NB).astype(jnp.int32)
    return jnp.zeros((NB,), jnp.int32).at[ordering].set(jnp.arange(NB, dtype=jnp.int32) // 2)


def draw_self_tiles(key, part):
    values = tile_values(jax.random.fold_in(key, 21), (NB, BS, BS))
    return (0.5 * (values + jnp.swapaxes(values, 1, 2))).astype(jnp.bfloat16)


def draw_link_tiles(key, part):
    partner = make_links(key)
    blocks = jnp.arange(NB, dtype=jnp.int32)[:, None]
    lower = jnp.minimum(blocks, partner)
    upper = jnp.maximum(blocks, partner)
    pair_id = (lower * NB + upper) * LINKS + jnp.arange(LINKS, dtype=jnp.int32)[None, :]
    tile_key = jax.random.fold_in(key, 31)

    def single(pair_number):
        return tile_values(jax.random.fold_in(tile_key, pair_number), (BS, BS))
    values = jax.vmap(jax.vmap(single))(pair_id)
    flipped = (blocks > partner)[:, :, None, None]
    return jnp.where(flipped, jnp.swapaxes(values, 2, 3), values).astype(jnp.bfloat16)


def vector_draw(key, salt):
    vector_key = jax.random.fold_in(key, salt)
    key_scale, key_noise = jax.random.split(vector_key, 2)
    node_scale = jnp.exp(jax.random.uniform(key_scale, (ROWS,), jnp.float32, 0.0, math.log(10.0)))
    noise = jnp.clip(jax.random.normal(key_noise, (K, ROWS), jnp.float32), -5.0, 5.0)
    return (noise * node_scale[None, :]).astype(jnp.float32)


def draw_vectors(key, part):
    return vector_draw(key, 51)


def draw_directions(key, part):
    return vector_draw(key, 61)


def setup_inputs(seed: int = 0) -> dict:
    keys = jax.random.split(jax.random.key(seed), 7)
    self_tiles = draw_self_tiles(jax.random.fold_in(keys[6], 71), 0)
    link_tiles = draw_link_tiles(jax.random.fold_in(keys[6], 71), 0)
    links = draw_links(jax.random.fold_in(keys[6], 71), 0)
    coarse_row = draw_coarse_row(jax.random.fold_in(keys[6], 71), 0)
    vectors = draw_vectors(jax.random.fold_in(keys[6], 71), 0)
    directions = draw_directions(jax.random.fold_in(keys[6], 71), 0)
    return {"self_tiles": self_tiles, "link_tiles": link_tiles, "links": links, "coarse_row": coarse_row, "vectors": vectors, "directions": directions}


spectral_shift = 0.25
damping = 0.6

def spd_solve(matrix, rhs):
    factor = jnp.linalg.cholesky(matrix)
    return jax.scipy.linalg.cho_solve((factor, True), rhs)

def operate(field, root_degree, self_tiles, link_tiles, links):
    scaled = (field / root_degree).astype(jnp.bfloat16)
    blocked = scaled.reshape(K, NB, BS).astype(jnp.float32)
    summed = jnp.einsum('kbj,bij->kbi', blocked, self_tiles.astype(jnp.float32))
    for link_slot in range(LINKS):
        remote = blocked[:, links[:, link_slot], :]
        summed = summed + jnp.einsum('kbj,bij->kbi', remote, link_tiles[:, link_slot].astype(jnp.float32))
    return field - summed.reshape(K, ROWS) / root_degree

def reference(self_tiles, link_tiles, links, coarse_row, vectors, directions):
    degree = (lax.optimization_barrier(jnp.sum(self_tiles.astype(jnp.float32), axis=2)) + lax.optimization_barrier(jnp.sum(link_tiles.astype(jnp.float32), axis=(1, 3)))).reshape(ROWS)
    root_degree = jnp.sqrt(degree)
    image_x = operate(vectors, root_degree, self_tiles, link_tiles, links)
    image_p = operate(directions, root_degree, self_tiles, link_tiles, links)
    gram_x = jnp.dot(vectors, vectors.T, precision=lax.Precision.HIGHEST)
    cross = jnp.dot(vectors, image_x.T, precision=lax.Precision.HIGHEST)
    ritz_coef = spd_solve(gram_x, cross)
    residual = image_x - jnp.dot(ritz_coef.T, vectors, precision=lax.Precision.HIGHEST)
    self_diag = jnp.diagonal(self_tiles, axis1=1, axis2=2).astype(jnp.float32).reshape(ROWS)
    diag_shift = 1.0 + spectral_shift - self_diag / degree
    first = damping * residual / diag_shift
    r_one = residual - (operate(first, root_degree, self_tiles, link_tiles, links) + spectral_shift * first)
    block_degree = degree.reshape(NB, BS).sum(axis=1)
    agg_degree = jnp.zeros((NC,), jnp.float32).at[coarse_row].add(block_degree)
    self_sum = lax.optimization_barrier(jnp.sum(self_tiles.astype(jnp.float32), axis=(1, 2)))
    link_sum = lax.optimization_barrier(jnp.sum(link_tiles.astype(jnp.float32), axis=(2, 3)))
    tile_sum = jnp.zeros((NC, NC), jnp.float32).at[coarse_row, coarse_row].add(self_sum)
    tile_sum = tile_sum.at[coarse_row[:, None], coarse_row[links]].add(link_sum)
    inv_scale = 1.0 / jnp.sqrt(agg_degree)
    coarse_matrix = ((1.0 + spectral_shift) * jnp.diag(agg_degree) - tile_sum) * inv_scale[:, None] * inv_scale[None, :]
    weighted = (root_degree * r_one).reshape(K, NB, BS).sum(axis=2)
    coarse_rhs = jnp.zeros((K, NC), jnp.float32).at[:, coarse_row].add(weighted) * inv_scale[None, :]
    coarse_error = spd_solve(coarse_matrix, coarse_rhs.T).T
    block_gain = (coarse_error * inv_scale[None, :])[:, coarse_row]
    second = first + (root_degree.reshape(NB, BS)[None] * block_gain[:, :, None]).reshape(K, ROWS)
    after = operate(second, root_degree, self_tiles, link_tiles, links) + spectral_shift * second
    corrected = second + damping * (residual - after) / diag_shift
    image_w = operate(corrected, root_degree, self_tiles, link_tiles, links)
    basis = jnp.concatenate([vectors, corrected, directions], axis=0)
    images = jnp.concatenate([image_x, image_w, image_p], axis=0)
    gram_b = jnp.dot(basis, basis.T, precision=lax.Precision.HIGHEST)
    gram_a = jnp.dot(basis, images.T, precision=lax.Precision.HIGHEST)
    factor = jnp.linalg.cholesky(gram_b)
    half_solved = jax.scipy.linalg.solve_triangular(factor, gram_a, lower=True)
    reduced = jax.scipy.linalg.solve_triangular(factor, half_solved.T, lower=True)
    projected = 0.5 * (reduced + reduced.T)
    return (residual, corrected, projected)
```

```python
import functools

import jax
import jax.numpy as jnp
from jax import lax
from jax.experimental import pallas as pl
from jax.experimental.pallas import tpu as pltpu
from jax.sharding import PartitionSpec as P

spectral_shift = 0.25
damping = 0.6
MESH = pl.DeviceIdType.MESH
F32 = jnp.float32

EX_GRAM_X, EX_CROSS, EX_RHS, EX_GRAM_B, EX_GRAM_A = range(5)
EX_XP, EX_W, EX_FINAL = range(3)


def dot_nt(a, b):
    return lax.dot_general(
        a, b, (((1,), (1,)), ((), ())), precision=lax.Precision.HIGHEST, preferred_element_type=F32
    )


def dot_nn(a, b):
    return lax.dot_general(
        a, b, (((1,), (0,)), ((), ())), precision=lax.Precision.HIGHEST, preferred_element_type=F32
    )


def tile_dot(a, tile):
    return lax.dot_general(a, tile, (((1,), (1,)), ((), ())), preferred_element_type=F32)


def iota(shape, axis):
    return lax.broadcasted_iota(jnp.int32, shape, axis)


def inverse(matrix):
    n = matrix.shape[0]
    eye = (iota((n, n), 0) == iota((n, n), 1)).astype(F32)
    both = jnp.concatenate([matrix, eye], axis=1)
    sub = iota((n, 2 * n), 0)
    if n <= 64:
        for k in range(n):
            row = both[k : k + 1, :] / both[k : k + 1, k : k + 1]
            both = jnp.where(sub == k, row, both - both[:, k : k + 1] * row)
    else:
        lane = iota((n, 2 * n), 1)

        def step(k, both):
            row = jnp.sum(jnp.where(sub == k, both, 0.0), axis=0, keepdims=True)
            col = jnp.sum(jnp.where(lane == k, both, 0.0), axis=1, keepdims=True)
            piv = jnp.sum(jnp.where(lane[:1] == k, row, 0.0), axis=1, keepdims=True)
            row = row / piv
            return jnp.where(sub == k, row, both - col * row)

        both = lax.fori_loop(0, n, step, both)
    return both[:, n:]


def inverse_factor(matrix):
    n = matrix.shape[0]
    sub = iota((n, n), 0)
    eye = sub == iota((n, n), 1)
    both = jnp.concatenate([matrix, eye.astype(F32)], axis=1)
    sub2 = iota((n, 1), 0)
    for k in range(n):
        row = both[k : k + 1, :] / both[k : k + 1, k : k + 1]
        col = jnp.where(sub2 > k, both[:, k : k + 1], 0.0)
        both = both - col * row
    pivots = jnp.sum(jnp.where(eye, both[:, :n], 0.0), axis=1, keepdims=True)
    return both[:, n:] / jnp.sqrt(pivots)


def kernel(
    n_rows,
    n_vec,
    self_hbm,
    link_hbm,
    links_s,
    coarse_s,
    links_v,
    coarse_v,
    vec_ref,
    dir_ref,
    res_ref,
    cor_ref,
    proj_ref,
    self_t,
    link_t,
    xp,
    wall,
    fin,
    win1,
    win2,
    win3,
    b_gx,
    b_cross,
    b_rhs,
    b_gb,
    b_ga,
    basis,
    deg,
    isq,
    dsh,
    rsb,
    rs,
    img,
    oht,
    first_r,
    rone_r,
    imw,
    load_sem,
    halo_send,
    halo_recv,
    row_send,
    row_recv,
    vec_send,
    vec_recv,
):
    r = lax.axis_index("rows")
    v = lax.axis_index("vec")
    bc, bs = self_t.shape[0], self_t.shape[1]
    slots = link_t.shape[1]
    vc, slab = vec_ref.shape
    kk = vc * n_vec
    nb = links_v.shape[0]
    nc = nb // 2
    lanes = b_gx.shape[2]

    loads = []
    for b in range(bc):
        loads.append(pltpu.make_async_copy(self_hbm.at[b], self_t.at[b], load_sem.at[0, b]))
        loads.append(pltpu.make_async_copy(link_hbm.at[b], link_t.at[b], load_sem.at[1, b]))
    for load in loads:
        load.start()

    barrier = pltpu.get_barrier_semaphore()

    def greet_rows(off, c):
        pl.semaphore_signal(
            barrier, inc=1, device_id={"rows": lax.rem(r + off, n_rows)}, device_id_type=MESH
        )
        return c

    def greet_vec(off, c):
        pl.semaphore_signal(
            barrier, inc=1, device_id={"vec": lax.rem(v + off, n_vec)}, device_id_type=MESH
        )
        return c

    lax.fori_loop(1, n_rows, greet_rows, 0, unroll=n_rows <= 16)
    lax.fori_loop(1, n_vec, greet_vec, 0, unroll=n_vec <= 16)

    def over(axis, e, buf, what):
        mine, count = (r, n_rows) if axis == "rows" else (v, n_vec)
        ssem, rsem = (row_send, row_recv) if axis == "rows" else (vec_send, vec_recv)

        def one(off, c):
            other = lax.rem(mine + off, count)
            slot = other if what == "recv" else mine
            copy = pltpu.make_async_remote_copy(
                src_ref=buf.at[slot],
                dst_ref=buf.at[slot],
                send_sem=ssem.at[e, other],
                recv_sem=rsem.at[e, slot],
                device_id={axis: other},
                device_id_type=MESH,
            )
            if what == "start":
                copy.start()
            elif what == "recv":
                copy.wait_recv()
            else:
                copy.wait_send()
            return c

        lax.fori_loop(1, count, one, 0, unroll=count <= 16)

    def halo(e, win, what):
        def copy(direction):
            return pltpu.make_async_remote_copy(
                src_ref=win.at[pl.ds(bc, bc)],
                dst_ref=win.at[pl.ds(0 if direction == 0 else 2 * bc, bc)],
                send_sem=halo_send.at[e, direction],
                recv_sem=halo_recv.at[e, direction],
                device_id={
                    "rows": lax.rem(r + (1 if direction == 0 else n_rows - 1), n_rows)
                },
                device_id_type=MESH,
            )

        has_next = r < n_rows - 1
        has_prev = r > 0
        for direction in range(2):
            sends = has_next if direction == 0 else has_prev
            gets = has_prev if direction == 0 else has_next
            if what == "start":
                pl.when(sends)(lambda d=direction: copy(d).start())
            elif what == "recv":
                pl.when(gets)(lambda d=direction: copy(d).wait_recv())
            else:
                pl.when(sends)(lambda d=direction: copy(d).wait_send())

    def blocks(body):
        def step(b, c):
            body(b, pl.ds(pl.multiple_of(b * bs, bs), bs))
            return c

        lax.fori_loop(0, bc, step, 0, unroll=True)

    xp[v, 0:vc, :] = vec_ref[...]
    xp[v, vc : 2 * vc, :] = dir_ref[...]
    pl.semaphore_wait(barrier, n_rows + n_vec - 2)
    over("vec", EX_XP, xp, "start")

    ones = jnp.ones((8, bs), jnp.bfloat16)
    for load in loads:
        load.wait()
    base = r * bc

    def degree_block(b, at):
        total = None
        for s in range(slots + 1):
            tile = self_t[b] if s == 0 else link_t[b, s - 1]
            sums = tile_dot(ones, tile)
            rsb[s, b] = sums
            rs[s, pl.ds(b, 1), :] = sums[0:1]
            total = sums if total is None else total + sums
        root = jnp.sqrt(total)
        deg[:, at] = root
        inv = 1.0 / root
        isq[:, at] = inv
        win1[bc + b] = xp[v, :, at] * inv

    blocks(degree_block)
    halo(0, win1, "start")

    lane8 = iota((bc, lanes), 1)
    tile_sums = jnp.zeros((bc, lanes), F32)
    block_degree = jnp.zeros((bc, 1), F32)
    for s in range(slots + 1):
        part = jnp.sum(rs[s], axis=1, keepdims=True)
        block_degree = block_degree + part
        tile_sums = jnp.where(lane8 == s, part, tile_sums)
    tile_sums = jnp.where(lane8 == slots + 1, block_degree, tile_sums)
    b_gx[r, pl.ds(kk, bc), :] = tile_sums

    def image1_self(b, at):
        img[:, at] = tile_dot(win1[bc + b].astype(jnp.bfloat16), self_t[b])

    blocks(image1_self)

    def diagonal_block(b, at):
        half = 128
        eye = iota((half, half), 0) == iota((half, half), 1)
        parts = []
        for h in range(bs // half):
            cut = self_t[b, h * half : (h + 1) * half, h * half : (h + 1) * half].astype(F32)
            parts.append(jnp.sum(jnp.where(eye, cut, 0.0), axis=0, keepdims=True))
        diag = jnp.concatenate(parts, axis=1)
        inv = isq[:, at]
        dsh[:, at] = damping / (1.0 + spectral_shift - diag * inv * inv)

    blocks(diagonal_block)

    lane_nc = iota((1, nc), 1)
    for s in range(slots + 1):
        for b in range(bc):
            target = base + b if s == 0 else links_s[base + b, s - 1]
            oht[s * bc + b : s * bc + b + 1, :] = (lane_nc == coarse_s[target]).astype(F32)

    over("vec", EX_XP, xp, "recv")
    for j in range(n_vec):
        basis[j * vc : (j + 1) * vc, :] = xp[j, 0:vc, :]
        basis[2 * kk + j * vc : 2 * kk + (j + 1) * vc, :] = xp[j, vc : 2 * vc, :]
    x_all = basis[0:kk, :]
    b_gx[r, 0:kk, 0:kk] = dot_nt(x_all, x_all)
    over("rows", EX_GRAM_X, b_gx, "start")

    def links_part(win, rows, out):
        def body(b, at):
            total = out[:, at]
            for s in range(slots):
                place = links_s[base + b, s] - base + bc
                remote = win[jnp.minimum(jnp.maximum(place, 0), 3 * bc - 1)]
                total = total + tile_dot(remote.astype(jnp.bfloat16), link_t[b, s])
            out[:, at] = total

        blocks(body)

    halo(0, win1, "recv")
    links_part(win1, 2 * vc, img)
    img[...] = xp[v] - img[...] * isq[...]
    b_cross[r, 0:vc, 0:kk] = dot_nt(img[0:vc, :], basis[0:kk, :])
    over("rows", EX_CROSS, b_cross, "start")

    over("rows", EX_GRAM_X, b_gx, "recv")
    got = jnp.sum(b_gx[:, 0:kk, 0:kk], axis=0)
    gram_inv = inverse(got)

    over("rows", EX_CROSS, b_cross, "recv")
    cross_t = jnp.sum(b_cross[:, :, 0:kk], axis=0)
    coef_t = dot_nn(cross_t, gram_inv)
    residual = img[0:vc, :] - dot_nn(coef_t, basis[0:kk, :])[0:vc]
    res_ref[...] = residual
    first = residual * dsh[0:vc, :]
    first_r[...] = first

    def put2(b, at):
        win2[bc + b] = first_r[:, at] * isq[0:vc, at]

    blocks(put2)
    halo(1, win2, "start")

    def image2_self(b, at):
        imw[:, at] = tile_dot(win2[bc + b].astype(jnp.bfloat16), self_t[b])

    blocks(image2_self)

    sums = b_gx[:, kk : kk + bc, :].reshape(nb, lanes)
    sub_b, lane_b = iota((nb, nb), 0), iota((nb, nb), 1)
    by_block = jnp.where(sub_b == lane_b, sums[:, 0:1], 0.0)
    for s in range(slots):
        by_block = by_block + jnp.where(links_v[:, s : s + 1] == lane_b, sums[:, s + 1 : s + 2], 0.0)
    pick = (iota((nc, nb), 0) == coarse_v[...]).astype(F32)
    tile_sum = dot_nn(pick, dot_nt(by_block, pick))
    agg = dot_nn(pick, sums)[:, slots + 1 : slots + 2]
    eye_c = iota((nc, nc), 0) == iota((nc, nc), 1)
    coarse = jnp.where(eye_c, (1.0 + spectral_shift) * agg, 0.0) - tile_sum
    to_gain = dot_nt(inverse(coarse), oht[...])

    halo(1, win2, "recv")
    links_part(win2, vc, imw)
    first = first_r[...]
    r_one = res_ref[...] - (1.0 + spectral_shift) * first + imw[...] * isq[0:vc, :]
    rone_r[...] = r_one
    weighted = r_one * deg[0:vc, :]
    rhs = jnp.zeros((vc, nc), F32)
    for b in range(bc):
        part = jnp.sum(weighted[:, b * bs : (b + 1) * bs], axis=1, keepdims=True)
        rhs = rhs + part * oht[b : b + 1, :]
    b_rhs[r, 0:vc, 0:nc] = rhs
    over("rows", EX_RHS, b_rhs, "start")
    over("rows", EX_RHS, b_rhs, "recv")
    gain = dot_nn(jnp.sum(b_rhs[:, :, 0:nc], axis=0), to_gain)[0:vc]

    def lift(b, at):
        moved = jnp.zeros((vc, bs), F32)
        for s in range(slots + 1):
            moved = moved + gain_at(s, b) * rsb[s, b][0:vc]
        inv = isq[0:vc, at]
        lifted = deg[0:vc, at] * gain_at(0, b)
        rest = rone_r[:, at] - (1.0 + spectral_shift) * lifted + moved * inv
        out = first_r[:, at] + lifted + rest * dsh[0:vc, at]
        cor_ref[:, at] = out
        win3[bc + b] = out * inv

    def gain_at(s, b):
        return gain[:, s * bc + b : s * bc + b + 1]

    for b in range(bc):
        lift(b, pl.ds(b * bs, bs))
    halo(2, win3, "start")
    wall[v] = cor_ref[...]
    over("vec", EX_W, wall, "start")

    def image3_self(b, at):
        imw[:, at] = tile_dot(win3[bc + b].astype(jnp.bfloat16), self_t[b])

    blocks(image3_self)

    over("vec", EX_W, wall, "recv")
    for j in range(n_vec):
        basis[kk + j * vc : kk + (j + 1) * vc, :] = wall[j]
    b_gb[r, :, 0 : 3 * kk] = dot_nt(basis[...], basis[...])
    over("rows", EX_GRAM_B, b_gb, "start")

    halo(2, win3, "recv")
    links_part(win3, vc, imw)
    imw[...] = cor_ref[...] - imw[...] * isq[0:vc, :]
    b_ga[r, 0 : 2 * vc, 0 : 3 * kk] = dot_nt(img[...], basis[...])
    b_ga[r, 2 * vc : 3 * vc, 0 : 3 * kk] = dot_nt(imw[...], basis[...])
    over("rows", EX_GRAM_A, b_ga, "start")

    over("rows", EX_GRAM_B, b_gb, "recv")
    linv = inverse_factor(jnp.sum(b_gb[:, :, 0 : 3 * kk], axis=0))

    over("rows", EX_GRAM_A, b_ga, "recv")
    gram_a_t = jnp.sum(b_ga[:, :, 0 : 3 * kk], axis=0)
    fin[v, :, 0 : 3 * kk] = dot_nt(gram_a_t, linv)
    over("vec", EX_FINAL, fin, "start")
    over("vec", EX_FINAL, fin, "recv")
    parts = (
        [fin[j, 0:vc, 0 : 3 * kk] for j in range(n_vec)]
        + [fin[j, 2 * vc : 3 * vc, 0 : 3 * kk] for j in range(n_vec)]
        + [fin[j, vc : 2 * vc, 0 : 3 * kk] for j in range(n_vec)]
    )
    for j, part in enumerate(parts):
        basis[j * vc : (j + 1) * vc, 0 : 3 * kk] = part
    reduced = dot_nn(linv, basis[:, 0 : 3 * kk])
    proj_ref[...] = 0.5 * (reduced + reduced.T)

    over("vec", EX_XP, xp, "sent")
    over("vec", EX_W, wall, "sent")
    over("vec", EX_FINAL, fin, "sent")
    over("rows", EX_GRAM_X, b_gx, "sent")
    over("rows", EX_CROSS, b_cross, "sent")
    over("rows", EX_RHS, b_rhs, "sent")
    over("rows", EX_GRAM_B, b_gb, "sent")
    over("rows", EX_GRAM_A, b_ga, "sent")
    halo(0, win1, "sent")
    halo(1, win2, "sent")
    halo(2, win3, "sent")


def body(n_rows, n_vec, self_tiles, link_tiles, links, coarse_row, vectors, directions):
    bc, bs = self_tiles.shape[:2]
    slots = link_tiles.shape[1]
    vc, slab = vectors.shape
    nb = links.shape[0]
    nc = nb // 2
    kk = vc * n_vec

    def up(x, m):
        return -(-x // m) * m

    lanes = 128
    basis_lanes = up(3 * kk, 128)
    vm = functools.partial(pl.BlockSpec, memory_space=pltpu.VMEM)
    sm = functools.partial(pl.BlockSpec, memory_space=pltpu.SMEM)
    scratch = [
        pltpu.VMEM((bc, bs, bs), jnp.bfloat16),
        pltpu.VMEM((bc, slots, bs, bs), jnp.bfloat16),
        pltpu.VMEM((n_vec, 2 * vc, slab), F32),
        pltpu.VMEM((n_vec, vc, slab), F32),
        pltpu.VMEM((n_vec, up(3 * vc, 8), basis_lanes), F32),
        pltpu.VMEM((3 * bc, 2 * vc, bs), F32),
        pltpu.VMEM((3 * bc, vc, bs), F32),
        pltpu.VMEM((3 * bc, vc, bs), F32),
        pltpu.VMEM((n_rows, kk + bc, lanes), F32),
        pltpu.VMEM((n_rows, up(vc, 8), up(kk, 128)), F32),
        pltpu.VMEM((n_rows, up(vc, 8), up(nc, 128)), F32),
        pltpu.VMEM((n_rows, 3 * kk, basis_lanes), F32),
        pltpu.VMEM((n_rows, up(3 * vc, 8), basis_lanes), F32),
        pltpu.VMEM((3 * kk, slab), F32),
        pltpu.VMEM((8, slab), F32),
        pltpu.VMEM((8, slab), F32),
        pltpu.VMEM((8, slab), F32),
        pltpu.VMEM((slots + 1, bc, 8, bs), F32),
        pltpu.VMEM((slots + 1, bc, bs), F32),
        pltpu.VMEM((2 * vc, slab), F32),
        pltpu.VMEM(((slots + 1) * bc, nc), F32),
        pltpu.VMEM((vc, slab), F32),
        pltpu.VMEM((vc, slab), F32),
        pltpu.VMEM((vc, slab), F32),
        pltpu.SemaphoreType.DMA((2, bc)),
        pltpu.SemaphoreType.DMA((3, 2)),
        pltpu.SemaphoreType.DMA((3, 2)),
        pltpu.SemaphoreType.DMA((5, n_rows)),
        pltpu.SemaphoreType.DMA((5, n_rows)),
        pltpu.SemaphoreType.DMA((3, n_vec)),
        pltpu.SemaphoreType.DMA((3, n_vec)),
    ]
    return pl.pallas_call(
        functools.partial(kernel, n_rows, n_vec),
        out_shape=(
            jax.ShapeDtypeStruct((vc, slab), F32),
            jax.ShapeDtypeStruct((vc, slab), F32),
            jax.ShapeDtypeStruct((3 * kk, 3 * kk), F32),
        ),
        in_specs=[
            pl.BlockSpec(memory_space=pl.ANY),
            pl.BlockSpec(memory_space=pl.ANY),
            sm(),
            sm(),
            vm(),
            vm(),
            vm(),
            vm(),
        ],
        out_specs=(vm(), vm(), vm()),
        scratch_shapes=scratch,
        compiler_params=pltpu.CompilerParams(
            collective_id=0, has_side_effects=True, vmem_limit_bytes=48 * 1024 * 1024
        ),
    )(
        self_tiles,
        link_tiles,
        links,
        coarse_row,
        links,
        coarse_row.reshape(1, nb),
        vectors,
        directions,
    )


def solution(mesh):
    in_specs = (
        P("rows", None, None),
        P("rows", None, None, None),
        P(),
        P(),
        P("vec", "rows"),
        P("vec", "rows"),
    )
    out_specs = (P("vec", "rows"), P("vec", "rows"), P())
    return jax.shard_map(
        functools.partial(body, mesh.shape["rows"], mesh.shape["vec"]),
        mesh=mesh,
        in_specs=in_specs,
        out_specs=out_specs,
        check_vma=False,
    )
```

```python
import functools

import jax
import jax.numpy as jnp
from jax import lax
from jax.experimental import pallas as pl
from jax.experimental.pallas import tpu as pltpu
from jax.sharding import PartitionSpec as P

spectral_shift = 0.25
damping = 0.6
MESH = pl.DeviceIdType.MESH
F32 = jnp.float32

EX_GRAM_X, EX_CROSS, EX_RHS, EX_GRAM_B, EX_GRAM_A = range(5)
EX_XP, EX_W, EX_FINAL = range(3)


def dot_nt(a, b):
    return lax.dot_general(
        a, b, (((1,), (1,)), ((), ())), precision=lax.Precision.HIGHEST, preferred_element_type=F32
    )


def dot_nn(a, b):
    return lax.dot_general(
        a, b, (((1,), (0,)), ((), ())), precision=lax.Precision.HIGHEST, preferred_element_type=F32
    )


def tile_dot(a, tile):
    return lax.dot_general(a, tile, (((1,), (1,)), ((), ())), preferred_element_type=F32)


def iota(shape, axis):
    return lax.broadcasted_iota(jnp.int32, shape, axis)


def eliminate(both, n, below_only):
    width = both.shape[1]
    sub = iota((n, width), 0)
    group = 4 if n % 4 == 0 else 1
    for k in range(0, n, group):
        cols = [jnp.broadcast_to(both[:, k + i : k + i + 1], (n, width)) for i in range(group)]
        ms, rows = [], []
        for i in range(group):
            at = k + i
            keep = sub > at if below_only else sub != at
            row = both[at : at + 1]
            for m, earlier in zip(ms, rows):
                row = row - m[at : at + 1] * earlier
            m = jnp.where(keep, cols[i] * (1.0 / cols[i][at : at + 1]), 0.0)
            for j in range(i + 1, group):
                cols[j] = cols[j] - m * cols[j][at : at + 1]
            ms.append(m)
            rows.append(row)
        for m, row in zip(ms, rows):
            both = both - m * row
    return both


def with_identity(matrix):
    n = matrix.shape[0]
    eye = iota((n, n), 0) == iota((n, n), 1)
    return jnp.concatenate([matrix, eye.astype(F32)], axis=1), eye


def inverse(matrix):
    n = matrix.shape[0]
    both, eye = with_identity(matrix)
    if n <= 64:
        both = eliminate(both, n, False)
    else:
        sub, lane = iota((n, 2 * n), 0), iota((n, 2 * n), 1)

        def step(k, both):
            row = jnp.sum(jnp.where(sub == k, both, 0.0), axis=0, keepdims=True)
            col = jnp.sum(jnp.where(lane == k, both, 0.0), axis=1, keepdims=True)
            piv = jnp.sum(jnp.where(lane[:1] == k, row, 0.0), axis=1, keepdims=True)
            return jnp.where(sub == k, row, both - col * (row / piv))

        both = lax.fori_loop(0, n, step, both)
    pivots = jnp.sum(jnp.where(eye, both[:, :n], 0.0), axis=1, keepdims=True)
    return both[:, n:] / pivots


def inverse_factor(matrix):
    n = matrix.shape[0]
    both, eye = with_identity(matrix)
    both = eliminate(both, n, True)
    pivots = jnp.sum(jnp.where(eye, both[:, :n], 0.0), axis=1, keepdims=True)
    return both[:, n:] / jnp.sqrt(pivots)


def kernel(
    n_rows,
    n_vec,
    self_hbm,
    link_hbm,
    links_hbm,
    coarse_hbm,
    vec_hbm,
    dir_hbm,
    res_ref,
    cor_ref,
    proj_ref,
    links_s,
    coarse_s,
    links_v,
    coarse_v,
    self_t,
    link_t,
    xp,
    wall,
    fin,
    win1,
    win2,
    win3,
    b_gx,
    b_cross,
    b_rhs,
    b_gb,
    b_ga,
    basis,
    deg,
    isq,
    dsh,
    rsb,
    rs,
    img,
    oht,
    first_r,
    rone_r,
    imw,
    load_sem,
    small_sem,
    halo_send,
    halo_recv,
    row_send,
    row_recv,
    vec_send,
    vec_recv,
):
    r = lax.axis_index("rows")
    v = lax.axis_index("vec")
    bc, bs = self_t.shape[0], self_t.shape[1]
    slots = link_t.shape[1]
    vc, slab = xp.shape[2:]
    kk = vc * n_vec
    nb = links_v.shape[1]
    nc = nb // 2
    lanes = b_gx.shape[2]

    small = [
        pltpu.make_async_copy(vec_hbm, xp.at[v, 0], small_sem.at[0]),
        pltpu.make_async_copy(dir_hbm, xp.at[v, 1], small_sem.at[1]),
        pltpu.make_async_copy(links_hbm, links_s, small_sem.at[2]),
        pltpu.make_async_copy(links_hbm, links_v, small_sem.at[3]),
        pltpu.make_async_copy(coarse_hbm, coarse_s, small_sem.at[4]),
        pltpu.make_async_copy(coarse_hbm, coarse_v, small_sem.at[5]),
    ]
    for load in small:
        load.start()

    def load_block(b):
        return (
            pltpu.make_async_copy(self_hbm.at[b], self_t.at[b], load_sem.at[0, b]),
            pltpu.make_async_copy(link_hbm.at[b], link_t.at[b], load_sem.at[1, b]),
        )

    for b in range(bc):
        for load in load_block(b):
            load.start()

    barrier = pltpu.get_barrier_semaphore()

    def greet_rows(off, c):
        pl.semaphore_signal(
            barrier, inc=1, device_id={"rows": lax.rem(r + off, n_rows)}, device_id_type=MESH
        )
        return c

    def greet_vec(off, c):
        pl.semaphore_signal(
            barrier, inc=1, device_id={"vec": lax.rem(v + off, n_vec)}, device_id_type=MESH
        )
        return c

    lax.fori_loop(1, n_rows, greet_rows, 0, unroll=n_rows <= 16)
    lax.fori_loop(1, n_vec, greet_vec, 0, unroll=n_vec <= 16)

    def over(axis, e, buf, what):
        mine, count = (r, n_rows) if axis == "rows" else (v, n_vec)
        ssem, rsem = (row_send, row_recv) if axis == "rows" else (vec_send, vec_recv)

        def one(off, c):
            other = lax.rem(mine + off, count)
            slot = other if what == "recv" else mine
            copy = pltpu.make_async_remote_copy(
                src_ref=buf.at[slot],
                dst_ref=buf.at[slot],
                send_sem=ssem.at[e, other],
                recv_sem=rsem.at[e, slot],
                device_id={axis: other},
                device_id_type=MESH,
            )
            if what == "start":
                copy.start()
            elif what == "recv":
                copy.wait_recv()
            else:
                copy.wait_send()
            return c

        lax.fori_loop(1, count, one, 0, unroll=count <= 16)

    def halo(e, win, what):
        def copy(direction):
            return pltpu.make_async_remote_copy(
                src_ref=win.at[pl.ds(bc, bc)],
                dst_ref=win.at[pl.ds(0 if direction == 0 else 2 * bc, bc)],
                send_sem=halo_send.at[e, direction],
                recv_sem=halo_recv.at[e, direction],
                device_id={
                    "rows": lax.rem(r + (1 if direction == 0 else n_rows - 1), n_rows)
                },
                device_id_type=MESH,
            )

        has_next = r < n_rows - 1
        has_prev = r > 0
        for direction in range(2):
            sends = has_next if direction == 0 else has_prev
            gets = has_prev if direction == 0 else has_next
            if what == "start":
                pl.when(sends)(lambda d=direction: copy(d).start())
            elif what == "recv":
                pl.when(gets)(lambda d=direction: copy(d).wait_recv())
            else:
                pl.when(sends)(lambda d=direction: copy(d).wait_send())

    def blocks(body):
        def step(b, c):
            body(b, pl.ds(pl.multiple_of(b * bs, bs), bs))
            return c

        lax.fori_loop(0, bc, step, 0, unroll=True)

    small[0].wait()
    small[1].wait()
    pl.semaphore_wait(barrier, n_rows + n_vec - 2)
    over("vec", EX_XP, xp, "start")

    ones = jnp.ones((8, bs), jnp.bfloat16)
    base = r * bc

    def degree_block(b, at):
        total = None
        for load in load_block(b):
            load.wait()
        for s in range(slots + 1):
            tile = self_t[b] if s == 0 else link_t[b, s - 1]
            sums = tile_dot(ones, tile)
            rsb[s, b] = sums
            rs[s, pl.ds(b, 1), :] = sums[0:1]
            total = sums if total is None else total + sums
        root = jnp.sqrt(total)
        deg[:, at] = root
        inv = 1.0 / root
        isq[:, at] = inv
        win1[bc + b, 0:vc] = xp[v, 0, :, at] * inv[0:vc]
        win1[bc + b, vc : 2 * vc] = xp[v, 1, :, at] * inv[0:vc]

    blocks(degree_block)
    halo(0, win1, "start")

    lane8 = iota((bc, lanes), 1)
    tile_sums = jnp.zeros((bc, lanes), F32)
    block_degree = jnp.zeros((bc, 1), F32)
    for s in range(slots + 1):
        part = jnp.sum(rs[s], axis=1, keepdims=True)
        block_degree = block_degree + part
        tile_sums = jnp.where(lane8 == s, part, tile_sums)
    tile_sums = jnp.where(lane8 == slots + 1, block_degree, tile_sums)
    b_gx[r, pl.ds(kk, bc), :] = tile_sums

    def image1_self(b, at):
        img[:, at] = tile_dot(win1[bc + b].astype(jnp.bfloat16), self_t[b])

    blocks(image1_self)

    def diagonal_block(b, at):
        half = 128
        eye = iota((half, half), 0) == iota((half, half), 1)
        parts = []
        for h in range(bs // half):
            cut = self_t[b, h * half : (h + 1) * half, h * half : (h + 1) * half].astype(F32)
            parts.append(jnp.sum(jnp.where(eye, cut, 0.0), axis=0, keepdims=True))
        diag = jnp.concatenate(parts, axis=1)
        inv = isq[:, at]
        dsh[:, at] = damping / (1.0 + spectral_shift - diag * inv * inv)

    blocks(diagonal_block)

    for load in small[2:]:
        load.wait()
    lane_nc = iota((1, nc), 1)
    for s in range(slots + 1):
        for b in range(bc):
            target = base + b if s == 0 else links_s[s - 1, base + b]
            oht[s * bc + b : s * bc + b + 1, :] = (lane_nc == coarse_s[0, target]).astype(F32)

    over("vec", EX_XP, xp, "recv")
    for j in range(n_vec):
        basis[j * vc : (j + 1) * vc, :] = xp[j, 0]
        basis[2 * kk + j * vc : 2 * kk + (j + 1) * vc, :] = xp[j, 1]
    x_all = basis[0:kk, :]
    b_gx[r, 0:kk, 0:kk] = dot_nt(x_all, x_all)
    over("rows", EX_GRAM_X, b_gx, "start")

    def links_part(win, rows, out):
        def body(b, at):
            total = out[:, at]
            for s in range(slots):
                place = links_s[s, base + b] - base + bc
                remote = win[jnp.minimum(jnp.maximum(place, 0), 3 * bc - 1)]
                total = total + tile_dot(remote.astype(jnp.bfloat16), link_t[b, s])
            out[:, at] = total

        blocks(body)

    halo(0, win1, "recv")
    links_part(win1, 2 * vc, img)
    img[0:vc, :] = xp[v, 0] - img[0:vc, :] * isq[0:vc, :]
    img[vc : 2 * vc, :] = xp[v, 1] - img[vc : 2 * vc, :] * isq[0:vc, :]
    b_cross[r, 0:vc, 0:kk] = dot_nt(img[0:vc, :], basis[0:kk, :])
    over("rows", EX_CROSS, b_cross, "start")

    over("rows", EX_GRAM_X, b_gx, "recv")
    got = jnp.sum(b_gx[:, 0:kk, 0:kk], axis=0)
    gram_inv = inverse(got)

    pick_sums = (iota((8, lanes), 0) == iota((8, lanes), 1)).astype(F32)
    sums = b_gx[:, kk : kk + bc, :].reshape(nb, lanes)
    sums_t = dot_nt(pick_sums, sums)
    sub_b, lane_b = iota((nb, nb), 0), iota((nb, nb), 1)
    by_block = jnp.where(sub_b == lane_b, sums_t[0:1], 0.0)
    for s in range(slots):
        by_block = by_block + jnp.where(links_v[s : s + 1] == sub_b, sums_t[s + 1 : s + 2], 0.0)
    pick = (iota((nc, nb), 0) == coarse_v[...]).astype(F32)
    tile_sum = dot_nt(dot_nt(pick, by_block), pick)
    agg = jnp.sum(pick * sums_t[slots + 1 : slots + 2], axis=1, keepdims=True)
    eye_c = iota((nc, nc), 0) == iota((nc, nc), 1)
    coarse = jnp.where(eye_c, (1.0 + spectral_shift) * agg, 0.0) - tile_sum
    to_gain = dot_nt(inverse(coarse), oht[...])

    over("rows", EX_CROSS, b_cross, "recv")
    cross_t = jnp.sum(b_cross[:, :, 0:kk], axis=0)
    coef_t = dot_nn(cross_t, gram_inv)
    residual = img[0:vc, :] - dot_nn(coef_t, basis[0:kk, :])[0:vc]
    res_ref[...] = residual
    first = residual * dsh[0:vc, :]
    first_r[...] = first

    def put2(b, at):
        win2[bc + b] = first_r[:, at] * isq[0:vc, at]

    blocks(put2)
    halo(1, win2, "start")

    def image2_self(b, at):
        imw[:, at] = tile_dot(win2[bc + b].astype(jnp.bfloat16), self_t[b])

    blocks(image2_self)

    halo(1, win2, "recv")
    links_part(win2, vc, imw)
    first = first_r[...]
    r_one = res_ref[...] - (1.0 + spectral_shift) * first + imw[...] * isq[0:vc, :]
    rone_r[...] = r_one
    weighted = r_one * deg[0:vc, :]
    rhs = jnp.zeros((vc, nc), F32)
    for b in range(bc):
        part = jnp.sum(weighted[:, b * bs : (b + 1) * bs], axis=1, keepdims=True)
        rhs = rhs + part * oht[b : b + 1, :]
    b_rhs[r, 0:vc, 0:nc] = rhs
    over("rows", EX_RHS, b_rhs, "start")
    over("rows", EX_RHS, b_rhs, "recv")
    gain = dot_nn(jnp.sum(b_rhs[:, :, 0:nc], axis=0), to_gain)[0:vc]

    def lift(b, at):
        moved = jnp.zeros((vc, bs), F32)
        for s in range(slots + 1):
            moved = moved + gain_at(s, b) * rsb[s, b][0:vc]
        inv = isq[0:vc, at]
        lifted = deg[0:vc, at] * gain_at(0, b)
        rest = rone_r[:, at] - (1.0 + spectral_shift) * lifted + moved * inv
        out = first_r[:, at] + lifted + rest * dsh[0:vc, at]
        cor_ref[:, at] = out
        win3[bc + b] = out * inv

    def gain_at(s, b):
        return gain[:, s * bc + b : s * bc + b + 1]

    for b in range(bc):
        lift(b, pl.ds(b * bs, bs))
    halo(2, win3, "start")
    wall[v] = cor_ref[...]
    over("vec", EX_W, wall, "start")

    def image3_self(b, at):
        imw[:, at] = tile_dot(win3[bc + b].astype(jnp.bfloat16), self_t[b])

    blocks(image3_self)

    over("vec", EX_W, wall, "recv")
    for j in range(n_vec):
        basis[kk + j * vc : kk + (j + 1) * vc, :] = wall[j]
    b_gb[r, :, 0 : 3 * kk] = dot_nt(basis[...], basis[...])
    over("rows", EX_GRAM_B, b_gb, "start")

    b_ga[r, 0 : 2 * vc, 0 : 3 * kk] = dot_nt(img[...], basis[...])
    halo(2, win3, "recv")
    links_part(win3, vc, imw)
    imw[...] = cor_ref[...] - imw[...] * isq[0:vc, :]
    b_ga[r, 2 * vc : 3 * vc, 0 : 3 * kk] = dot_nt(imw[...], basis[...])
    over("rows", EX_GRAM_A, b_ga, "start")

    over("rows", EX_GRAM_B, b_gb, "recv")
    linv = inverse_factor(jnp.sum(b_gb[:, :, 0 : 3 * kk], axis=0))

    over("rows", EX_GRAM_A, b_ga, "recv")
    gram_a_t = jnp.sum(b_ga[:, :, 0 : 3 * kk], axis=0)
    fin[v, :, 0 : 3 * kk] = dot_nt(gram_a_t, linv)
    over("vec", EX_FINAL, fin, "start")
    over("vec", EX_FINAL, fin, "recv")
    parts = (
        [fin[j, 0:vc, 0 : 3 * kk] for j in range(n_vec)]
        + [fin[j, 2 * vc : 3 * vc, 0 : 3 * kk] for j in range(n_vec)]
        + [fin[j, vc : 2 * vc, 0 : 3 * kk] for j in range(n_vec)]
    )
    for j, part in enumerate(parts):
        basis[j * vc : (j + 1) * vc, 0 : 3 * kk] = part
    reduced = dot_nn(linv, basis[:, 0 : 3 * kk])
    proj_ref[...] = 0.5 * (reduced + reduced.T)

    over("vec", EX_XP, xp, "sent")
    over("vec", EX_W, wall, "sent")
    over("vec", EX_FINAL, fin, "sent")
    over("rows", EX_GRAM_X, b_gx, "sent")
    over("rows", EX_CROSS, b_cross, "sent")
    over("rows", EX_RHS, b_rhs, "sent")
    over("rows", EX_GRAM_B, b_gb, "sent")
    over("rows", EX_GRAM_A, b_ga, "sent")
    halo(0, win1, "sent")
    halo(1, win2, "sent")
    halo(2, win3, "sent")


def body(n_rows, n_vec, self_tiles, link_tiles, links, coarse_row, vectors, directions):
    bc, bs = self_tiles.shape[:2]
    slots = link_tiles.shape[1]
    vc, slab = vectors.shape
    nb = links.shape[0]
    nc = nb // 2
    kk = vc * n_vec

    def up(x, m):
        return -(-x // m) * m

    lanes = 128
    basis_lanes = up(3 * kk, 128)
    vm = functools.partial(pl.BlockSpec, memory_space=pltpu.VMEM)
    scratch = [
        pltpu.SMEM((slots, nb), jnp.int32),
        pltpu.SMEM((1, nb), jnp.int32),
        pltpu.VMEM((slots, nb), jnp.int32),
        pltpu.VMEM((1, nb), jnp.int32),
        pltpu.VMEM((bc, bs, bs), jnp.bfloat16),
        pltpu.VMEM((bc, slots, bs, bs), jnp.bfloat16),
        pltpu.VMEM((n_vec, 2, vc, slab), F32),
        pltpu.VMEM((n_vec, vc, slab), F32),
        pltpu.VMEM((n_vec, up(3 * vc, 8), basis_lanes), F32),
        pltpu.VMEM((3 * bc, 2 * vc, bs), F32),
        pltpu.VMEM((3 * bc, vc, bs), F32),
        pltpu.VMEM((3 * bc, vc, bs), F32),
        pltpu.VMEM((n_rows, kk + bc, lanes), F32),
        pltpu.VMEM((n_rows, up(vc, 8), up(kk, 128)), F32),
        pltpu.VMEM((n_rows, up(vc, 8), up(nc, 128)), F32),
        pltpu.VMEM((n_rows, 3 * kk, basis_lanes), F32),
        pltpu.VMEM((n_rows, up(3 * vc, 8), basis_lanes), F32),
        pltpu.VMEM((3 * kk, slab), F32),
        pltpu.VMEM((8, slab), F32),
        pltpu.VMEM((8, slab), F32),
        pltpu.VMEM((8, slab), F32),
        pltpu.VMEM((slots + 1, bc, 8, bs), F32),
        pltpu.VMEM((slots + 1, bc, bs), F32),
        pltpu.VMEM((2 * vc, slab), F32),
        pltpu.VMEM(((slots + 1) * bc, nc), F32),
        pltpu.VMEM((vc, slab), F32),
        pltpu.VMEM((vc, slab), F32),
        pltpu.VMEM((vc, slab), F32),
        pltpu.SemaphoreType.DMA((2, bc)),
        pltpu.SemaphoreType.DMA((6,)),
        pltpu.SemaphoreType.DMA((3, 2)),
        pltpu.SemaphoreType.DMA((3, 2)),
        pltpu.SemaphoreType.DMA((5, n_rows)),
        pltpu.SemaphoreType.DMA((5, n_rows)),
        pltpu.SemaphoreType.DMA((3, n_vec)),
        pltpu.SemaphoreType.DMA((3, n_vec)),
    ]
    return pl.pallas_call(
        functools.partial(kernel, n_rows, n_vec),
        out_shape=(
            jax.ShapeDtypeStruct((vc, slab), F32),
            jax.ShapeDtypeStruct((vc, slab), F32),
            jax.ShapeDtypeStruct((3 * kk, 3 * kk), F32),
        ),
        in_specs=[pl.BlockSpec(memory_space=pltpu.HBM)] * 6,
        out_specs=(vm(), vm(), vm()),
        scratch_shapes=scratch,
        compiler_params=pltpu.CompilerParams(
            collective_id=0, has_side_effects=True, vmem_limit_bytes=48 * 1024 * 1024
        ),
    )(
        self_tiles,
        link_tiles,
        links.T,
        coarse_row.reshape(1, nb),
        vectors,
        directions,
    )


def solution(mesh):
    in_specs = (
        P("rows", None, None),
        P("rows", None, None, None),
        P(),
        P(),
        P("vec", "rows"),
        P("vec", "rows"),
    )
    out_specs = (P("vec", "rows"), P("vec", "rows"), P())
    return jax.shard_map(
        functools.partial(body, mesh.shape["rows"], mesh.shape["vec"]),
        mesh=mesh,
        in_specs=in_specs,
        out_specs=out_specs,
        check_vma=False,
    )
```

```python
import functools

import jax
import jax.numpy as jnp
from jax import lax
from jax.experimental import pallas as pl
from jax.experimental.pallas import tpu as pltpu
from jax.sharding import PartitionSpec as P

spectral_shift = 0.25
damping = 0.6
MESH = pl.DeviceIdType.MESH
F32 = jnp.float32

EX_GRAM_X, EX_CROSS, EX_RHS, EX_GRAM_B, EX_GRAM_A = range(5)
EX_XP, EX_W, EX_FINAL = range(3)


def dot_nt(a, b):
    return lax.dot_general(
        a, b, (((1,), (1,)), ((), ())), precision=lax.Precision.HIGHEST, preferred_element_type=F32
    )


def dot_nn(a, b):
    return lax.dot_general(
        a, b, (((1,), (0,)), ((), ())), precision=lax.Precision.HIGHEST, preferred_element_type=F32
    )


def tile_dot(tile, rows):
    return lax.dot_general(tile, rows, (((1,), (1,)), ((), ())), preferred_element_type=F32)


def in_slot(rows, b, count):
    zero = jnp.zeros((8, rows.shape[1]), F32)
    if rows.shape[0] < 8:
        rows = jnp.concatenate([rows, zero[rows.shape[0] :]], axis=0)
    parts = [zero] * b + [rows] + [zero] * (count - 1 - b)
    return jnp.concatenate(parts, axis=0).astype(jnp.bfloat16)


def iota(shape, axis):
    return lax.broadcasted_iota(jnp.int32, shape, axis)


def eliminate(both, n, below_only):
    width = both.shape[1]
    sub = iota((n, width), 0)
    group = 4 if n % 4 == 0 else 1
    for k in range(0, n, group):
        cols = [jnp.broadcast_to(both[:, k + i : k + i + 1], (n, width)) for i in range(group)]
        ms, rows = [], []
        for i in range(group):
            at = k + i
            keep = sub > at if below_only else sub != at
            row = both[at : at + 1]
            for m, earlier in zip(ms, rows):
                row = row - m[at : at + 1] * earlier
            m = jnp.where(keep, cols[i] * (1.0 / cols[i][at : at + 1]), 0.0)
            for j in range(i + 1, group):
                cols[j] = cols[j] - m * cols[j][at : at + 1]
            ms.append(m)
            rows.append(row)
        for m, row in zip(ms, rows):
            both = both - m * row
    return both


def with_identity(matrix):
    n = matrix.shape[0]
    eye = iota((n, n), 0) == iota((n, n), 1)
    return jnp.concatenate([matrix, eye.astype(F32)], axis=1), eye


def inverse(matrix):
    n = matrix.shape[0]
    both, eye = with_identity(matrix)
    if n <= 64:
        both = eliminate(both, n, False)
    else:
        sub, lane = iota((n, 2 * n), 0), iota((n, 2 * n), 1)

        def step(k, both):
            row = jnp.sum(jnp.where(sub == k, both, 0.0), axis=0, keepdims=True)
            col = jnp.sum(jnp.where(lane == k, both, 0.0), axis=1, keepdims=True)
            piv = jnp.sum(jnp.where(lane[:1] == k, row, 0.0), axis=1, keepdims=True)
            return jnp.where(sub == k, row, both - col * (row / piv))

        both = lax.fori_loop(0, n, step, both)
    pivots = jnp.sum(jnp.where(eye, both[:, :n], 0.0), axis=1, keepdims=True)
    return both[:, n:] / pivots


def inverse_factor(matrix):
    n = matrix.shape[0]
    both, eye = with_identity(matrix)
    both = eliminate(both, n, True)
    pivots = jnp.sum(jnp.where(eye, both[:, :n], 0.0), axis=1, keepdims=True)
    return both[:, n:] / jnp.sqrt(pivots)


def kernel(
    n_rows,
    n_vec,
    self_hbm,
    link_hbm,
    links_hbm,
    coarse_hbm,
    vec_hbm,
    dir_hbm,
    res_ref,
    cor_ref,
    proj_ref,
    links_s,
    coarse_s,
    links_v,
    coarse_v,
    self_t,
    link_t,
    xp,
    wall,
    fin,
    win1,
    win2,
    win3,
    b_gx,
    b_cross,
    b_rhs,
    b_gb,
    b_ga,
    basis,
    deg,
    isq,
    dsh,
    rs,
    img,
    oht,
    first_r,
    rone_r,
    imw,
    load_sem,
    small_sem,
    halo_send,
    halo_recv,
    row_send,
    row_recv,
    vec_send,
    vec_recv,
):
    r = lax.axis_index("rows")
    v = lax.axis_index("vec")
    bc, bs = self_t.shape[0], self_t.shape[1]
    slots = link_t.shape[1]
    vc, slab = xp.shape[2:]
    kk = vc * n_vec
    nb = links_v.shape[1]
    nc = nb // 2
    lanes = b_gx.shape[2]

    small = [
        pltpu.make_async_copy(vec_hbm, xp.at[v, 0], small_sem.at[0]),
        pltpu.make_async_copy(dir_hbm, xp.at[v, 1], small_sem.at[1]),
        pltpu.make_async_copy(links_hbm, links_s, small_sem.at[2]),
        pltpu.make_async_copy(links_hbm, links_v, small_sem.at[3]),
        pltpu.make_async_copy(coarse_hbm, coarse_s, small_sem.at[4]),
        pltpu.make_async_copy(coarse_hbm, coarse_v, small_sem.at[5]),
    ]
    for load in small:
        load.start()

    def load_block(b):
        return (
            pltpu.make_async_copy(self_hbm.at[b], self_t.at[b], load_sem.at[0, b]),
            pltpu.make_async_copy(link_hbm.at[b], link_t.at[b], load_sem.at[1, b]),
        )

    for b in range(bc):
        for load in load_block(b):
            load.start()

    barrier = pltpu.get_barrier_semaphore()

    def greet_rows(off, c):
        pl.semaphore_signal(
            barrier, inc=1, device_id={"rows": lax.rem(r + off, n_rows)}, device_id_type=MESH
        )
        return c

    def greet_vec(off, c):
        pl.semaphore_signal(
            barrier, inc=1, device_id={"vec": lax.rem(v + off, n_vec)}, device_id_type=MESH
        )
        return c

    lax.fori_loop(1, n_rows, greet_rows, 0, unroll=n_rows <= 16)
    lax.fori_loop(1, n_vec, greet_vec, 0, unroll=n_vec <= 16)

    def over(axis, e, buf, what):
        mine, count = (r, n_rows) if axis == "rows" else (v, n_vec)
        ssem, rsem = (row_send, row_recv) if axis == "rows" else (vec_send, vec_recv)

        def one(off, c):
            other = lax.rem(mine + off, count)
            slot = other if what == "recv" else mine
            copy = pltpu.make_async_remote_copy(
                src_ref=buf.at[slot],
                dst_ref=buf.at[slot],
                send_sem=ssem.at[e, other],
                recv_sem=rsem.at[e, slot],
                device_id={axis: other},
                device_id_type=MESH,
            )
            if what == "start":
                copy.start()
            elif what == "recv":
                copy.wait_recv()
            else:
                copy.wait_send()
            return c

        lax.fori_loop(1, count, one, 0, unroll=count <= 16)

    def halo(e, win, what):
        def copy(direction):
            return pltpu.make_async_remote_copy(
                src_ref=win.at[pl.ds(bc, bc)],
                dst_ref=win.at[pl.ds(0 if direction == 0 else 2 * bc, bc)],
                send_sem=halo_send.at[e, direction],
                recv_sem=halo_recv.at[e, direction],
                device_id={
                    "rows": lax.rem(r + (1 if direction == 0 else n_rows - 1), n_rows)
                },
                device_id_type=MESH,
            )

        has_next = r < n_rows - 1
        has_prev = r > 0
        for direction in range(2):
            sends = has_next if direction == 0 else has_prev
            gets = has_prev if direction == 0 else has_next
            if what == "start":
                pl.when(sends)(lambda d=direction: copy(d).start())
            elif what == "recv":
                pl.when(gets)(lambda d=direction: copy(d).wait_recv())
            else:
                pl.when(sends)(lambda d=direction: copy(d).wait_send())

    def blocks(body):
        def step(b, c):
            body(b, pl.ds(pl.multiple_of(b * bs, bs), bs))
            return c

        lax.fori_loop(0, bc, step, 0, unroll=True)

    small[0].wait()
    small[1].wait()
    pl.semaphore_wait(barrier, n_rows + n_vec - 2)
    over("vec", EX_XP, xp, "start")

    base = r * bc
    tiles = (slots + 1) * bc
    total = jnp.zeros((bs, tiles), F32)
    tile_row = iota((tiles, bs), 0)
    for b in range(bc):
        for load in load_block(b):
            load.wait()
        for s in range(slots + 1):
            tile = self_t[b] if s == 0 else link_t[b, s - 1]
            one = jnp.where(tile_row == s * bc + b, 1.0, 0.0).astype(jnp.bfloat16)
            total = total + tile_dot(tile, one)
    rs[...] = total.T
    degree = rs[0:bc]
    for s in range(1, slots + 1):
        degree = degree + rs[s * bc : (s + 1) * bc]
    root = jnp.sqrt(degree)
    inv_root = 1.0 / root
    for b in range(bc):
        at = slice(b * bs, (b + 1) * bs)
        inv = jnp.broadcast_to(inv_root[b : b + 1], (8, bs))
        deg[:, at] = jnp.broadcast_to(root[b : b + 1], (8, bs))
        isq[:, at] = inv
        win1[bc + b, 0:vc] = xp[v, 0, :, at] * inv[0:vc]
        win1[bc + b, vc : 2 * vc] = xp[v, 1, :, at] * inv[0:vc]

    halo(0, win1, "start")

    lane8 = iota((bc, lanes), 1)
    tile_sums = jnp.zeros((bc, lanes), F32)
    block_degree = jnp.zeros((bc, 1), F32)
    for s in range(slots + 1):
        part = jnp.sum(rs[s * bc : (s + 1) * bc], axis=1, keepdims=True)
        block_degree = block_degree + part
        tile_sums = jnp.where(lane8 == s, part, tile_sums)
    tile_sums = jnp.where(lane8 == slots + 1, block_degree, tile_sums)
    b_gx[r, pl.ds(kk, bc), :] = tile_sums

    def self_part(win):
        total = jnp.zeros((bs, 8 * bc), F32)
        for b in range(bc):
            total = total + tile_dot(self_t[b], in_slot(win[bc + b], b, bc))
        return total

    def links_part(win, total):
        for b in range(bc):
            for s in range(slots):
                place = links_s[s, base + b] - base + bc
                remote = win[jnp.minimum(jnp.maximum(place, 0), 3 * bc - 1)]
                total = total + tile_dot(link_t[b, s], in_slot(remote, b, bc))
        return total.T

    image1 = self_part(win1)

    def diagonal_block(b, at):
        half = 128
        eye = iota((half, half), 0) == iota((half, half), 1)
        parts = []
        for h in range(bs // half):
            cut = self_t[b, h * half : (h + 1) * half, h * half : (h + 1) * half].astype(F32)
            parts.append(jnp.sum(jnp.where(eye, cut, 0.0), axis=0, keepdims=True))
        diag = jnp.concatenate(parts, axis=1)
        inv = isq[:, at]
        dsh[:, at] = damping / (1.0 + spectral_shift - diag * inv * inv)

    blocks(diagonal_block)

    for load in small[2:]:
        load.wait()
    lane_nc = iota((1, nc), 1)
    for s in range(slots + 1):
        for b in range(bc):
            target = base + b if s == 0 else links_s[s - 1, base + b]
            oht[s * bc + b : s * bc + b + 1, :] = (lane_nc == coarse_s[0, target]).astype(F32)

    over("vec", EX_XP, xp, "recv")
    for j in range(n_vec):
        basis[j * vc : (j + 1) * vc, :] = xp[j, 0]
        basis[2 * kk + j * vc : 2 * kk + (j + 1) * vc, :] = xp[j, 1]
    x_all = basis[0:kk, :]
    b_gx[r, 0:kk, 0:kk] = dot_nt(x_all, x_all)
    over("rows", EX_GRAM_X, b_gx, "start")

    halo(0, win1, "recv")
    image1 = links_part(win1, image1)
    for b in range(bc):
        at = slice(b * bs, (b + 1) * bs)
        adj = image1[8 * b : 8 * b + 8] * isq[:, at]
        img[0:vc, at] = xp[v, 0, :, at] - adj[0:vc]
        img[vc : 2 * vc, at] = xp[v, 1, :, at] - adj[vc : 2 * vc]
    b_cross[r, 0:vc, 0:kk] = dot_nt(img[0:vc, :], basis[0:kk, :])
    over("rows", EX_CROSS, b_cross, "start")

    over("rows", EX_GRAM_X, b_gx, "recv")
    got = jnp.sum(b_gx[:, 0:kk, 0:kk], axis=0)
    gram_inv = inverse(got)

    pick_sums = (iota((8, lanes), 0) == iota((8, lanes), 1)).astype(F32)
    sums = b_gx[:, kk : kk + bc, :].reshape(nb, lanes)
    sums_t = dot_nt(pick_sums, sums)
    sub_b, lane_b = iota((nb, nb), 0), iota((nb, nb), 1)
    by_block = jnp.where(sub_b == lane_b, sums_t[0:1], 0.0)
    for s in range(slots):
        by_block = by_block + jnp.where(links_v[s : s + 1] == sub_b, sums_t[s + 1 : s + 2], 0.0)
    pick = (iota((nc, nb), 0) == coarse_v[...]).astype(F32)
    tile_sum = dot_nt(dot_nt(pick, by_block), pick)
    agg = jnp.sum(pick * sums_t[slots + 1 : slots + 2], axis=1, keepdims=True)
    eye_c = iota((nc, nc), 0) == iota((nc, nc), 1)
    coarse = jnp.where(eye_c, (1.0 + spectral_shift) * agg, 0.0) - tile_sum
    to_gain = dot_nt(inverse(coarse), oht[...])

    over("rows", EX_CROSS, b_cross, "recv")
    cross_t = jnp.sum(b_cross[:, :, 0:kk], axis=0)
    coef_t = dot_nn(cross_t, gram_inv)
    residual = img[0:vc, :] - dot_nn(coef_t, basis[0:kk, :])[0:vc]
    res_ref[...] = residual
    first = residual * dsh[0:vc, :]
    first_r[...] = first

    def put2(b, at):
        win2[bc + b] = first_r[:, at] * isq[0:vc, at]

    blocks(put2)
    halo(1, win2, "start")

    image2 = self_part(win2)

    halo(1, win2, "recv")
    image2 = links_part(win2, image2)
    for b in range(bc):
        imw[:, b * bs : (b + 1) * bs] = image2[8 * b : 8 * b + vc]
    first = first_r[...]
    r_one = res_ref[...] - (1.0 + spectral_shift) * first + imw[...] * isq[0:vc, :]
    rone_r[...] = r_one
    weighted = r_one * deg[0:vc, :]
    rhs = jnp.zeros((vc, nc), F32)
    for b in range(bc):
        part = jnp.sum(weighted[:, b * bs : (b + 1) * bs], axis=1, keepdims=True)
        rhs = rhs + part * oht[b : b + 1, :]
    b_rhs[r, 0:vc, 0:nc] = rhs
    over("rows", EX_RHS, b_rhs, "start")
    over("rows", EX_RHS, b_rhs, "recv")
    gain = dot_nn(jnp.sum(b_rhs[:, :, 0:nc], axis=0), to_gain)[0:vc]

    def lift(b, at):
        moved = jnp.zeros((vc, bs), F32)
        for s in range(slots + 1):
            moved = moved + gain_at(s, b) * rs[s * bc + b : s * bc + b + 1]
        inv = isq[0:vc, at]
        lifted = deg[0:vc, at] * gain_at(0, b)
        rest = rone_r[:, at] - (1.0 + spectral_shift) * lifted + moved * inv
        out = first_r[:, at] + lifted + rest * dsh[0:vc, at]
        cor_ref[:, at] = out
        win3[bc + b] = out * inv

    def gain_at(s, b):
        return gain[:, s * bc + b : s * bc + b + 1]

    for b in range(bc):
        lift(b, pl.ds(b * bs, bs))
    halo(2, win3, "start")
    wall[v] = cor_ref[...]
    over("vec", EX_W, wall, "start")

    image3 = self_part(win3)

    over("vec", EX_W, wall, "recv")
    for j in range(n_vec):
        basis[kk + j * vc : kk + (j + 1) * vc, :] = wall[j]
    b_gb[r, :, 0 : 3 * kk] = dot_nt(basis[...], basis[...])
    over("rows", EX_GRAM_B, b_gb, "start")

    b_ga[r, 0 : 2 * vc, 0 : 3 * kk] = dot_nt(img[...], basis[...])
    halo(2, win3, "recv")
    image3 = links_part(win3, image3)
    for b in range(bc):
        imw[:, b * bs : (b + 1) * bs] = image3[8 * b : 8 * b + vc]
    imw[...] = cor_ref[...] - imw[...] * isq[0:vc, :]
    b_ga[r, 2 * vc : 3 * vc, 0 : 3 * kk] = dot_nt(imw[...], basis[...])
    over("rows", EX_GRAM_A, b_ga, "start")

    over("rows", EX_GRAM_B, b_gb, "recv")
    linv = inverse_factor(jnp.sum(b_gb[:, :, 0 : 3 * kk], axis=0))

    over("rows", EX_GRAM_A, b_ga, "recv")
    gram_a_t = jnp.sum(b_ga[:, :, 0 : 3 * kk], axis=0)
    fin[v, :, 0 : 3 * kk] = dot_nt(gram_a_t, linv)
    over("vec", EX_FINAL, fin, "start")
    over("vec", EX_FINAL, fin, "recv")
    parts = (
        [fin[j, 0:vc, 0 : 3 * kk] for j in range(n_vec)]
        + [fin[j, 2 * vc : 3 * vc, 0 : 3 * kk] for j in range(n_vec)]
        + [fin[j, vc : 2 * vc, 0 : 3 * kk] for j in range(n_vec)]
    )
    for j, part in enumerate(parts):
        basis[j * vc : (j + 1) * vc, 0 : 3 * kk] = part
    reduced = dot_nn(linv, basis[:, 0 : 3 * kk])
    proj_ref[...] = 0.5 * (reduced + reduced.T)

    over("vec", EX_XP, xp, "sent")
    over("vec", EX_W, wall, "sent")
    over("vec", EX_FINAL, fin, "sent")
    over("rows", EX_GRAM_X, b_gx, "sent")
    over("rows", EX_CROSS, b_cross, "sent")
    over("rows", EX_RHS, b_rhs, "sent")
    over("rows", EX_GRAM_B, b_gb, "sent")
    over("rows", EX_GRAM_A, b_ga, "sent")
    halo(0, win1, "sent")
    halo(1, win2, "sent")
    halo(2, win3, "sent")


def body(n_rows, n_vec, self_tiles, link_tiles, links, coarse_row, vectors, directions):
    bc, bs = self_tiles.shape[:2]
    slots = link_tiles.shape[1]
    vc, slab = vectors.shape
    nb = links.shape[0]
    nc = nb // 2
    kk = vc * n_vec

    def up(x, m):
        return -(-x // m) * m

    lanes = 128
    basis_lanes = up(3 * kk, 128)
    vm = functools.partial(pl.BlockSpec, memory_space=pltpu.VMEM)
    scratch = [
        pltpu.SMEM((slots, nb), jnp.int32),
        pltpu.SMEM((1, nb), jnp.int32),
        pltpu.VMEM((slots, nb), jnp.int32),
        pltpu.VMEM((1, nb), jnp.int32),
        pltpu.VMEM((bc, bs, bs), jnp.bfloat16),
        pltpu.VMEM((bc, slots, bs, bs), jnp.bfloat16),
        pltpu.VMEM((n_vec, 2, vc, slab), F32),
        pltpu.VMEM((n_vec, vc, slab), F32),
        pltpu.VMEM((n_vec, up(3 * vc, 8), basis_lanes), F32),
        pltpu.VMEM((3 * bc, 2 * vc, bs), F32),
        pltpu.VMEM((3 * bc, vc, bs), F32),
        pltpu.VMEM((3 * bc, vc, bs), F32),
        pltpu.VMEM((n_rows, kk + bc, lanes), F32),
        pltpu.VMEM((n_rows, up(vc, 8), up(kk, 128)), F32),
        pltpu.VMEM((n_rows, up(vc, 8), up(nc, 128)), F32),
        pltpu.VMEM((n_rows, 3 * kk, basis_lanes), F32),
        pltpu.VMEM((n_rows, up(3 * vc, 8), basis_lanes), F32),
        pltpu.VMEM((3 * kk, slab), F32),
        pltpu.VMEM((8, slab), F32),
        pltpu.VMEM((8, slab), F32),
        pltpu.VMEM((8, slab), F32),
        pltpu.VMEM(((slots + 1) * bc, bs), F32),
        pltpu.VMEM((2 * vc, slab), F32),
        pltpu.VMEM(((slots + 1) * bc, nc), F32),
        pltpu.VMEM((vc, slab), F32),
        pltpu.VMEM((vc, slab), F32),
        pltpu.VMEM((vc, slab), F32),
        pltpu.SemaphoreType.DMA((2, bc)),
        pltpu.SemaphoreType.DMA((6,)),
        pltpu.SemaphoreType.DMA((3, 2)),
        pltpu.SemaphoreType.DMA((3, 2)),
        pltpu.SemaphoreType.DMA((5, n_rows)),
        pltpu.SemaphoreType.DMA((5, n_rows)),
        pltpu.SemaphoreType.DMA((3, n_vec)),
        pltpu.SemaphoreType.DMA((3, n_vec)),
    ]
    return pl.pallas_call(
        functools.partial(kernel, n_rows, n_vec),
        out_shape=(
            jax.ShapeDtypeStruct((vc, slab), F32),
            jax.ShapeDtypeStruct((vc, slab), F32),
            jax.ShapeDtypeStruct((3 * kk, 3 * kk), F32),
        ),
        in_specs=[pl.BlockSpec(memory_space=pltpu.HBM)] * 6,
        out_specs=(vm(), vm(), vm()),
        scratch_shapes=scratch,
        compiler_params=pltpu.CompilerParams(
            collective_id=0, has_side_effects=True, vmem_limit_bytes=63 * 1024 * 1024
        ),
    )(
        self_tiles,
        link_tiles,
        links.T,
        coarse_row.reshape(1, nb),
        vectors,
        directions,
    )


def solution(mesh):
    in_specs = (
        P("rows", None, None),
        P("rows", None, None, None),
        P(),
        P(),
        P("vec", "rows"),
        P("vec", "rows"),
    )
    out_specs = (P("vec", "rows"), P("vec", "rows"), P())
    return jax.shard_map(
        functools.partial(body, mesh.shape["rows"], mesh.shape["vec"]),
        mesh=mesh,
        in_specs=in_specs,
        out_specs=out_specs,
        check_vma=False,
    )
```

```python
import functools

import jax
import jax.numpy as jnp
from jax import lax
from jax.experimental import pallas as pl
from jax.experimental.pallas import tpu as pltpu
from jax.sharding import PartitionSpec as P

spectral_shift = 0.25
damping = 0.6
MESH = pl.DeviceIdType.MESH
F32 = jnp.float32

EX_GRAM_X, EX_CROSS, EX_RHS, EX_GRAM_B, EX_GRAM_A = range(5)
EX_XP, EX_W, EX_FINAL = range(3)


def dot_nt(a, b):
    return lax.dot_general(
        a, b, (((1,), (1,)), ((), ())), precision=lax.Precision.HIGHEST, preferred_element_type=F32
    )


def dot_nn(a, b):
    return lax.dot_general(
        a, b, (((1,), (0,)), ((), ())), precision=lax.Precision.HIGHEST, preferred_element_type=F32
    )


def tile_dot(tile, rows):
    return lax.dot_general(tile, rows, (((1,), (1,)), ((), ())), preferred_element_type=F32)


def in_slot(rows, b, count):
    zero = jnp.zeros((8, rows.shape[1]), F32)
    if rows.shape[0] < 8:
        rows = jnp.concatenate([rows, zero[rows.shape[0] :]], axis=0)
    parts = [zero] * b + [rows] + [zero] * (count - 1 - b)
    return jnp.concatenate(parts, axis=0).astype(jnp.bfloat16)


def iota(shape, axis):
    return lax.broadcasted_iota(jnp.int32, shape, axis)


def eliminate(both, n, below_only):
    width = both.shape[1]
    sub = iota((n, width), 0)
    group = 4 if n % 4 == 0 else 1
    for k in range(0, n, group):
        cols = [jnp.broadcast_to(both[:, k + i : k + i + 1], (n, width)) for i in range(group)]
        ms, rows = [], []
        for i in range(group):
            at = k + i
            keep = sub > at if below_only else sub != at
            row = both[at : at + 1]
            for m, earlier in zip(ms, rows):
                row = row - m[at : at + 1] * earlier
            m = jnp.where(keep, cols[i] * (1.0 / cols[i][at : at + 1]), 0.0)
            for j in range(i + 1, group):
                cols[j] = cols[j] - m * cols[j][at : at + 1]
            ms.append(m)
            rows.append(row)
        for m, row in zip(ms, rows):
            both = both - m * row
    return both


def with_identity(matrix):
    n = matrix.shape[0]
    eye = iota((n, n), 0) == iota((n, n), 1)
    return jnp.concatenate([matrix, eye.astype(F32)], axis=1), eye


def inverse(matrix):
    n = matrix.shape[0]
    both, eye = with_identity(matrix)
    if n <= 64:
        both = eliminate(both, n, False)
    else:
        sub, lane = iota((n, 2 * n), 0), iota((n, 2 * n), 1)

        def step(k, both):
            row = jnp.sum(jnp.where(sub == k, both, 0.0), axis=0, keepdims=True)
            col = jnp.sum(jnp.where(lane == k, both, 0.0), axis=1, keepdims=True)
            piv = jnp.sum(jnp.where(lane[:1] == k, row, 0.0), axis=1, keepdims=True)
            return jnp.where(sub == k, row, both - col * (row / piv))

        both = lax.fori_loop(0, n, step, both)
    pivots = jnp.sum(jnp.where(eye, both[:, :n], 0.0), axis=1, keepdims=True)
    return both[:, n:] / pivots


def inverse_factor(matrix):
    n = matrix.shape[0]
    both, eye = with_identity(matrix)
    both = eliminate(both, n, True)
    pivots = jnp.sum(jnp.where(eye, both[:, :n], 0.0), axis=1, keepdims=True)
    return both[:, n:] / jnp.sqrt(pivots)


def kernel(
    n_rows,
    n_vec,
    self_hbm,
    link_hbm,
    links_hbm,
    coarse_hbm,
    vec_hbm,
    dir_hbm,
    res_hbm,
    cor_hbm,
    proj_hbm,
    res_ref,
    cor_ref,
    proj_ref,
    links_s,
    coarse_s,
    links_v,
    coarse_v,
    self_t,
    link_t,
    xp,
    wall,
    fin,
    win1,
    win2,
    win3,
    b_gx,
    b_cross,
    b_rhs,
    b_gb,
    b_ga,
    basis,
    deg,
    isq,
    dsh,
    rs,
    img,
    oht,
    first_r,
    rone_r,
    imw,
    load_sem,
    small_sem,
    halo_send,
    halo_recv,
    row_send,
    row_recv,
    vec_send,
    vec_recv,
):
    r = lax.axis_index("rows")
    v = lax.axis_index("vec")
    bc, bs = self_t.shape[0], self_t.shape[1]
    slots = link_t.shape[1]
    vc, slab = xp.shape[2:]
    kk = vc * n_vec
    nb = links_v.shape[1]
    nc = nb // 2
    lanes = b_gx.shape[2]

    small = [
        pltpu.make_async_copy(vec_hbm, xp.at[v, 0], small_sem.at[0]),
        pltpu.make_async_copy(dir_hbm, xp.at[v, 1], small_sem.at[1]),
        pltpu.make_async_copy(links_hbm, links_s, small_sem.at[2]),
        pltpu.make_async_copy(links_hbm, links_v, small_sem.at[3]),
        pltpu.make_async_copy(coarse_hbm, coarse_s, small_sem.at[4]),
        pltpu.make_async_copy(coarse_hbm, coarse_v, small_sem.at[5]),
    ]
    for load in small:
        load.start()

    def load_block(b):
        return (
            pltpu.make_async_copy(self_hbm.at[b], self_t.at[b], load_sem.at[0, b]),
            pltpu.make_async_copy(link_hbm.at[b], link_t.at[b], load_sem.at[1, b]),
        )

    for b in range(bc):
        for load in load_block(b):
            load.start()

    barrier = pltpu.get_barrier_semaphore()

    def greet_rows(off, c):
        pl.semaphore_signal(
            barrier, inc=1, device_id={"rows": lax.rem(r + off, n_rows)}, device_id_type=MESH
        )
        return c

    def greet_vec(off, c):
        pl.semaphore_signal(
            barrier, inc=1, device_id={"vec": lax.rem(v + off, n_vec)}, device_id_type=MESH
        )
        return c

    lax.fori_loop(1, n_rows, greet_rows, 0, unroll=n_rows <= 16)
    lax.fori_loop(1, n_vec, greet_vec, 0, unroll=n_vec <= 16)

    def over(axis, e, buf, what):
        mine, count = (r, n_rows) if axis == "rows" else (v, n_vec)
        ssem, rsem = (row_send, row_recv) if axis == "rows" else (vec_send, vec_recv)

        def one(off, c):
            other = lax.rem(mine + off, count)
            slot = other if what == "recv" else mine
            copy = pltpu.make_async_remote_copy(
                src_ref=buf.at[slot],
                dst_ref=buf.at[slot],
                send_sem=ssem.at[e, other],
                recv_sem=rsem.at[e, slot],
                device_id={axis: other},
                device_id_type=MESH,
            )
            if what == "start":
                copy.start()
            elif what == "recv":
                copy.wait_recv()
            else:
                copy.wait_send()
            return c

        lax.fori_loop(1, count, one, 0, unroll=count <= 16)

    def halo(e, win, what):
        def copy(direction):
            return pltpu.make_async_remote_copy(
                src_ref=win.at[pl.ds(bc, bc)],
                dst_ref=win.at[pl.ds(0 if direction == 0 else 2 * bc, bc)],
                send_sem=halo_send.at[e, direction],
                recv_sem=halo_recv.at[e, direction],
                device_id={
                    "rows": lax.rem(r + (1 if direction == 0 else n_rows - 1), n_rows)
                },
                device_id_type=MESH,
            )

        has_next = r < n_rows - 1
        has_prev = r > 0
        for direction in range(2):
            sends = has_next if direction == 0 else has_prev
            gets = has_prev if direction == 0 else has_next
            if what == "start":
                pl.when(sends)(lambda d=direction: copy(d).start())
            elif what == "recv":
                pl.when(gets)(lambda d=direction: copy(d).wait_recv())
            else:
                pl.when(sends)(lambda d=direction: copy(d).wait_send())

    def blocks(body):
        def step(b, c):
            body(b, pl.ds(pl.multiple_of(b * bs, bs), bs))
            return c

        lax.fori_loop(0, bc, step, 0, unroll=True)

    base = r * bc
    tiles = (slots + 1) * bc
    total = jnp.zeros((bs, tiles), F32)
    tile_row = iota((tiles, bs), 0)
    for b in range(bc):
        for load in load_block(b):
            load.wait()
        for s in range(slots + 1):
            tile = self_t[b] if s == 0 else link_t[b, s - 1]
            one = jnp.where(tile_row == s * bc + b, 1.0, 0.0).astype(jnp.bfloat16)
            total = total + tile_dot(tile, one)
    rs[...] = total.T
    degree = rs[0:bc]
    for s in range(1, slots + 1):
        degree = degree + rs[s * bc : (s + 1) * bc]
    small[0].wait()
    small[1].wait()
    root = jnp.sqrt(degree)
    inv_root = 1.0 / root
    for b in range(bc):
        at = slice(b * bs, (b + 1) * bs)
        inv = jnp.broadcast_to(inv_root[b : b + 1], (8, bs))
        deg[:, at] = jnp.broadcast_to(root[b : b + 1], (8, bs))
        isq[:, at] = inv
        win1[bc + b, 0:vc] = xp[v, 0, :, at] * inv[0:vc]
        win1[bc + b, vc : 2 * vc] = xp[v, 1, :, at] * inv[0:vc]

    pl.semaphore_wait(barrier, n_rows + n_vec - 2)
    halo(0, win1, "start")
    over("vec", EX_XP, xp, "start")

    lane8 = iota((bc, lanes), 1)
    tile_sums = jnp.zeros((bc, lanes), F32)
    block_degree = jnp.zeros((bc, 1), F32)
    for s in range(slots + 1):
        part = jnp.sum(rs[s * bc : (s + 1) * bc], axis=1, keepdims=True)
        block_degree = block_degree + part
        tile_sums = jnp.where(lane8 == s, part, tile_sums)
    tile_sums = jnp.where(lane8 == slots + 1, block_degree, tile_sums)
    b_gx[r, pl.ds(kk, bc), :] = tile_sums

    def self_part(win):
        total = jnp.zeros((bs, 8 * bc), F32)
        for b in range(bc):
            total = total + tile_dot(self_t[b], in_slot(win[bc + b], b, bc))
        return total

    def links_part(win, total):
        for b in range(bc):
            for s in range(slots):
                place = links_s[s, base + b] - base + bc
                remote = win[jnp.minimum(jnp.maximum(place, 0), 3 * bc - 1)]
                total = total + tile_dot(link_t[b, s], in_slot(remote, b, bc))
        return total.T

    image1 = self_part(win1)

    def diagonal_block(b, at):
        half = 128
        eye = iota((half, half), 0) == iota((half, half), 1)
        parts = []
        for h in range(bs // half):
            cut = self_t[b, h * half : (h + 1) * half, h * half : (h + 1) * half].astype(F32)
            parts.append(jnp.sum(jnp.where(eye, cut, 0.0), axis=0, keepdims=True))
        diag = jnp.concatenate(parts, axis=1)
        inv = isq[:, at]
        dsh[:, at] = damping / (1.0 + spectral_shift - diag * inv * inv)

    blocks(diagonal_block)

    for load in small[2:]:
        load.wait()
    lane_nc = iota((1, nc), 1)
    for s in range(slots + 1):
        for b in range(bc):
            target = base + b if s == 0 else links_s[s - 1, base + b]
            oht[s * bc + b : s * bc + b + 1, :] = (lane_nc == coarse_s[0, target]).astype(F32)

    over("vec", EX_XP, xp, "recv")
    for j in range(n_vec):
        basis[j * vc : (j + 1) * vc, :] = xp[j, 0]
        basis[2 * kk + j * vc : 2 * kk + (j + 1) * vc, :] = xp[j, 1]
    x_all = basis[0:kk, :]
    b_gx[r, 0:kk, 0:kk] = dot_nt(x_all, x_all)
    over("rows", EX_GRAM_X, b_gx, "start")

    halo(0, win1, "recv")
    image1 = links_part(win1, image1)
    for b in range(bc):
        at = slice(b * bs, (b + 1) * bs)
        adj = image1[8 * b : 8 * b + 8] * isq[:, at]
        img[0:vc, at] = xp[v, 0, :, at] - adj[0:vc]
        img[vc : 2 * vc, at] = xp[v, 1, :, at] - adj[vc : 2 * vc]
    b_cross[r, 0:vc, 0:kk] = dot_nt(img[0:vc, :], basis[0:kk, :])
    over("rows", EX_CROSS, b_cross, "start")

    over("rows", EX_GRAM_X, b_gx, "recv")
    got = jnp.sum(b_gx[:, 0:kk, 0:kk], axis=0)
    gram_inv = inverse(got)

    pick_sums = (iota((8, lanes), 0) == iota((8, lanes), 1)).astype(F32)
    sums = b_gx[:, kk : kk + bc, :].reshape(nb, lanes)
    sums_t = dot_nt(pick_sums, sums)
    sub_b, lane_b = iota((nb, nb), 0), iota((nb, nb), 1)
    by_block = jnp.where(sub_b == lane_b, sums_t[0:1], 0.0)
    for s in range(slots):
        by_block = by_block + jnp.where(links_v[s : s + 1] == sub_b, sums_t[s + 1 : s + 2], 0.0)
    pick = (iota((nc, nb), 0) == coarse_v[...]).astype(F32)
    tile_sum = dot_nt(dot_nt(pick, by_block), pick)
    agg = jnp.sum(pick * sums_t[slots + 1 : slots + 2], axis=1, keepdims=True)
    eye_c = iota((nc, nc), 0) == iota((nc, nc), 1)
    coarse = jnp.where(eye_c, (1.0 + spectral_shift) * agg, 0.0) - tile_sum
    to_gain = dot_nt(inverse(coarse), oht[...])

    over("rows", EX_CROSS, b_cross, "recv")
    cross_t = jnp.sum(b_cross[:, :, 0:kk], axis=0)
    coef_t = dot_nn(cross_t, gram_inv)
    residual = img[0:vc, :] - dot_nn(coef_t, basis[0:kk, :])[0:vc]
    res_ref[...] = residual
    out_res = pltpu.make_async_copy(res_ref, res_hbm, small_sem.at[6])
    out_res.start()
    first = residual * dsh[0:vc, :]
    first_r[...] = first

    def put2(b, at):
        win2[bc + b] = first_r[:, at] * isq[0:vc, at]

    blocks(put2)
    halo(1, win2, "start")

    rhs = jnp.zeros((vc, nc), F32)
    direct = (res_ref[...] - (1.0 + spectral_shift) * first) * deg[0:vc, :]
    for b in range(bc):
        sent = win2[bc + b].astype(jnp.bfloat16).astype(F32)
        for s in range(slots + 1):
            t = s * bc + b
            terms = sent * rs[t : t + 1]
            if s == 0:
                terms = terms + direct[:, b * bs : (b + 1) * bs]
            rhs = rhs + jnp.sum(terms, axis=1, keepdims=True) * oht[t : t + 1, :]
    b_rhs[r, 0:vc, 0:nc] = rhs
    over("rows", EX_RHS, b_rhs, "start")

    image2 = self_part(win2)

    halo(1, win2, "recv")
    image2 = links_part(win2, image2)
    for b in range(bc):
        imw[:, b * bs : (b + 1) * bs] = image2[8 * b : 8 * b + vc]
    first = first_r[...]
    r_one = res_ref[...] - (1.0 + spectral_shift) * first + imw[...] * isq[0:vc, :]
    rone_r[...] = r_one
    over("rows", EX_RHS, b_rhs, "recv")
    gain = dot_nn(jnp.sum(b_rhs[:, :, 0:nc], axis=0), to_gain)[0:vc]

    def lift(b, at):
        moved = jnp.zeros((vc, bs), F32)
        for s in range(slots + 1):
            moved = moved + gain_at(s, b) * rs[s * bc + b : s * bc + b + 1]
        inv = isq[0:vc, at]
        lifted = deg[0:vc, at] * gain_at(0, b)
        rest = rone_r[:, at] - (1.0 + spectral_shift) * lifted + moved * inv
        out = first_r[:, at] + lifted + rest * dsh[0:vc, at]
        cor_ref[:, at] = out
        win3[bc + b] = out * inv

    def gain_at(s, b):
        return gain[:, s * bc + b : s * bc + b + 1]

    for b in range(bc):
        lift(b, pl.ds(b * bs, bs))
    halo(2, win3, "start")
    out_cor = pltpu.make_async_copy(cor_ref, cor_hbm, small_sem.at[7])
    out_cor.start()
    wall[v] = cor_ref[...]
    over("vec", EX_W, wall, "start")

    image3 = self_part(win3)

    over("vec", EX_W, wall, "recv")
    for j in range(n_vec):
        basis[kk + j * vc : kk + (j + 1) * vc, :] = wall[j]
    b_gb[r, :, 0 : 3 * kk] = dot_nt(basis[...], basis[...])
    over("rows", EX_GRAM_B, b_gb, "start")

    b_ga[r, 0 : 2 * vc, 0 : 3 * kk] = dot_nt(img[...], basis[...])
    halo(2, win3, "recv")
    image3 = links_part(win3, image3)
    for b in range(bc):
        imw[:, b * bs : (b + 1) * bs] = image3[8 * b : 8 * b + vc]
    imw[...] = cor_ref[...] - imw[...] * isq[0:vc, :]
    b_ga[r, 2 * vc : 3 * vc, 0 : 3 * kk] = dot_nt(imw[...], basis[...])
    over("rows", EX_GRAM_A, b_ga, "start")

    over("rows", EX_GRAM_B, b_gb, "recv")
    linv = inverse_factor(jnp.sum(b_gb[:, :, 0 : 3 * kk], axis=0))

    over("rows", EX_GRAM_A, b_ga, "recv")
    gram_a_t = jnp.sum(b_ga[:, :, 0 : 3 * kk], axis=0)
    fin[v, :, 0 : 3 * kk] = dot_nt(gram_a_t, linv)
    over("vec", EX_FINAL, fin, "start")
    over("vec", EX_FINAL, fin, "recv")
    parts = (
        [fin[j, 0:vc, 0 : 3 * kk] for j in range(n_vec)]
        + [fin[j, 2 * vc : 3 * vc, 0 : 3 * kk] for j in range(n_vec)]
        + [fin[j, vc : 2 * vc, 0 : 3 * kk] for j in range(n_vec)]
    )
    for j, part in enumerate(parts):
        basis[j * vc : (j + 1) * vc, 0 : 3 * kk] = part
    reduced = dot_nn(linv, basis[:, 0 : 3 * kk])
    proj_ref[...] = 0.5 * (reduced + reduced.T)
    out_proj = pltpu.make_async_copy(proj_ref, proj_hbm, small_sem.at[8])
    out_proj.start()

    over("vec", EX_XP, xp, "sent")
    over("vec", EX_W, wall, "sent")
    over("vec", EX_FINAL, fin, "sent")
    over("rows", EX_GRAM_X, b_gx, "sent")
    over("rows", EX_CROSS, b_cross, "sent")
    over("rows", EX_RHS, b_rhs, "sent")
    over("rows", EX_GRAM_B, b_gb, "sent")
    over("rows", EX_GRAM_A, b_ga, "sent")
    halo(0, win1, "sent")
    halo(1, win2, "sent")
    halo(2, win3, "sent")
    out_res.wait()
    out_cor.wait()
    out_proj.wait()


def body(n_rows, n_vec, self_tiles, link_tiles, links, coarse_row, vectors, directions):
    bc, bs = self_tiles.shape[:2]
    slots = link_tiles.shape[1]
    vc, slab = vectors.shape
    nb = links.shape[0]
    nc = nb // 2
    kk = vc * n_vec

    def up(x, m):
        return -(-x // m) * m

    lanes = 128
    basis_lanes = up(3 * kk, 128)
    hbm = pl.BlockSpec(memory_space=pltpu.HBM)
    scratch = [
        pltpu.VMEM((vc, slab), F32),
        pltpu.VMEM((vc, slab), F32),
        pltpu.VMEM((3 * kk, 3 * kk), F32),
        pltpu.SMEM((slots, nb), jnp.int32),
        pltpu.SMEM((1, nb), jnp.int32),
        pltpu.VMEM((slots, nb), jnp.int32),
        pltpu.VMEM((1, nb), jnp.int32),
        pltpu.VMEM((bc, bs, bs), jnp.bfloat16),
        pltpu.VMEM((bc, slots, bs, bs), jnp.bfloat16),
        pltpu.VMEM((n_vec, 2, vc, slab), F32),
        pltpu.VMEM((n_vec, vc, slab), F32),
        pltpu.VMEM((n_vec, up(3 * vc, 8), basis_lanes), F32),
        pltpu.VMEM((3 * bc, 2 * vc, bs), F32),
        pltpu.VMEM((3 * bc, vc, bs), F32),
        pltpu.VMEM((3 * bc, vc, bs), F32),
        pltpu.VMEM((n_rows, kk + bc, lanes), F32),
        pltpu.VMEM((n_rows, up(vc, 8), up(kk, 128)), F32),
        pltpu.VMEM((n_rows, up(vc, 8), up(nc, 128)), F32),
        pltpu.VMEM((n_rows, 3 * kk, basis_lanes), F32),
        pltpu.VMEM((n_rows, up(3 * vc, 8), basis_lanes), F32),
        pltpu.VMEM((3 * kk, slab), F32),
        pltpu.VMEM((8, slab), F32),
        pltpu.VMEM((8, slab), F32),
        pltpu.VMEM((8, slab), F32),
        pltpu.VMEM(((slots + 1) * bc, bs), F32),
        pltpu.VMEM((2 * vc, slab), F32),
        pltpu.VMEM(((slots + 1) * bc, nc), F32),
        pltpu.VMEM((vc, slab), F32),
        pltpu.VMEM((vc, slab), F32),
        pltpu.VMEM((vc, slab), F32),
        pltpu.SemaphoreType.DMA((2, bc)),
        pltpu.SemaphoreType.DMA((9,)),
        pltpu.SemaphoreType.DMA((3, 2)),
        pltpu.SemaphoreType.DMA((3, 2)),
        pltpu.SemaphoreType.DMA((5, n_rows)),
        pltpu.SemaphoreType.DMA((5, n_rows)),
        pltpu.SemaphoreType.DMA((3, n_vec)),
        pltpu.SemaphoreType.DMA((3, n_vec)),
    ]
    out_shape = (
        jax.ShapeDtypeStruct((vc, slab), F32),
        jax.ShapeDtypeStruct((vc, slab), F32),
        jax.ShapeDtypeStruct((3 * kk, 3 * kk), F32),
    )
    results = pl.pallas_call(
        functools.partial(kernel, n_rows, n_vec),
        out_shape=out_shape,
        in_specs=[hbm] * 6,
        out_specs=(hbm, hbm, hbm),
        scratch_shapes=scratch,
        compiler_params=pltpu.CompilerParams(
            collective_id=0, has_side_effects=True, vmem_limit_bytes=63 * 1024 * 1024
        ),
    )(
        self_tiles,
        link_tiles,
        links.T,
        coarse_row.reshape(1, nb),
        vectors,
        directions,
    )
    return pl.pallas_call(
        hand_over,
        out_shape=out_shape,
        in_specs=[hbm] * 3,
        out_specs=(hbm, hbm, hbm),
        scratch_shapes=[pltpu.SemaphoreType.DMA((3,))],
        compiler_params=pltpu.CompilerParams(vmem_limit_bytes=63 * 1024 * 1024),
    )(*results)


def hand_over(a, b, c, out_a, out_b, out_c, sem):
    copies = [
        pltpu.make_async_copy(a, out_a, sem.at[0]),
        pltpu.make_async_copy(b, out_b, sem.at[1]),
        pltpu.make_async_copy(c, out_c, sem.at[2]),
    ]
    for copy in copies:
        copy.start()
    for copy in copies:
        copy.wait()


def solution(mesh):
    in_specs = (
        P("rows", None, None),
        P("rows", None, None, None),
        P(),
        P(),
        P("vec", "rows"),
        P("vec", "rows"),
    )
    out_specs = (P("vec", "rows"), P("vec", "rows"), P())
    return jax.shard_map(
        functools.partial(body, mesh.shape["rows"], mesh.shape["vec"]),
        mesh=mesh,
        in_specs=in_specs,
        out_specs=out_specs,
        check_vma=False,
    )
```

```python
import functools

import jax
import jax.numpy as jnp
from jax import lax
from jax.experimental import pallas as pl
from jax.experimental.pallas import tpu as pltpu
from jax.sharding import PartitionSpec as P

spectral_shift = 0.25
damping = 0.6
MESH = pl.DeviceIdType.MESH
F32 = jnp.float32

EX_GRAM_X, EX_CROSS, EX_RHS, EX_GRAM_B, EX_GRAM_A = range(5)
EX_XP, EX_W, EX_FINAL = range(3)


def dot_nt(a, b):
    return lax.dot_general(
        a, b, (((1,), (1,)), ((), ())), precision=lax.Precision.HIGHEST, preferred_element_type=F32
    )


def dot_nn(a, b):
    return lax.dot_general(
        a, b, (((1,), (0,)), ((), ())), precision=lax.Precision.HIGHEST, preferred_element_type=F32
    )


def tile_dot(tile, rows):
    return lax.dot_general(tile, rows, (((1,), (1,)), ((), ())), preferred_element_type=F32)


def in_slot(rows, b, count):
    zero = jnp.zeros((8, rows.shape[1]), F32)
    if rows.shape[0] < 8:
        rows = jnp.concatenate([rows, zero[rows.shape[0] :]], axis=0)
    parts = [zero] * b + [rows] + [zero] * (count - 1 - b)
    return jnp.concatenate(parts, axis=0).astype(jnp.bfloat16)


def iota(shape, axis):
    return lax.broadcasted_iota(jnp.int32, shape, axis)


def eliminate(both, n, below_only):
    width = both.shape[1]
    sub = iota((n, width), 0)
    group = 4 if n % 4 == 0 else 1
    for k in range(0, n, group):
        cols = [jnp.broadcast_to(both[:, k + i : k + i + 1], (n, width)) for i in range(group)]
        ms, rows = [], []
        for i in range(group):
            at = k + i
            keep = sub > at if below_only else sub != at
            row = both[at : at + 1]
            for m, earlier in zip(ms, rows):
                row = row - m[at : at + 1] * earlier
            m = jnp.where(keep, cols[i] * (1.0 / cols[i][at : at + 1]), 0.0)
            for j in range(i + 1, group):
                cols[j] = cols[j] - m * cols[j][at : at + 1]
            ms.append(m)
            rows.append(row)
        for m, row in zip(ms, rows):
            both = both - m * row
    return both


def with_identity(matrix):
    n = matrix.shape[0]
    eye = iota((n, n), 0) == iota((n, n), 1)
    return jnp.concatenate([matrix, eye.astype(F32)], axis=1), eye


def inverse(matrix):
    n = matrix.shape[0]
    both, eye = with_identity(matrix)
    if n <= 64:
        both = eliminate(both, n, False)
    else:
        sub, lane = iota((n, 2 * n), 0), iota((n, 2 * n), 1)

        def step(k, both):
            row = jnp.sum(jnp.where(sub == k, both, 0.0), axis=0, keepdims=True)
            col = jnp.sum(jnp.where(lane == k, both, 0.0), axis=1, keepdims=True)
            piv = jnp.sum(jnp.where(lane[:1] == k, row, 0.0), axis=1, keepdims=True)
            return jnp.where(sub == k, row, both - col * (row / piv))

        both = lax.fori_loop(0, n, step, both)
    pivots = jnp.sum(jnp.where(eye, both[:, :n], 0.0), axis=1, keepdims=True)
    return both[:, n:] / pivots


def inverse_factor(matrix):
    n = matrix.shape[0]
    both, eye = with_identity(matrix)
    both = eliminate(both, n, True)
    pivots = jnp.sum(jnp.where(eye, both[:, :n], 0.0), axis=1, keepdims=True)
    return both[:, n:] / jnp.sqrt(pivots)


def kernel(
    n_rows,
    n_vec,
    self_hbm,
    link_hbm,
    links_hbm,
    coarse_hbm,
    vec_hbm,
    dir_hbm,
    res_hbm,
    cor_hbm,
    proj_hbm,
    res_ref,
    cor_ref,
    proj_ref,
    links_s,
    coarse_s,
    links_v,
    coarse_v,
    self_t,
    link_t,
    xp,
    wall,
    fin,
    win1,
    win2,
    win3,
    b_gx,
    b_cross,
    b_rhs,
    b_gb,
    b_ga,
    basis,
    deg,
    isq,
    dsh,
    rs,
    img,
    oht,
    first_r,
    rone_r,
    imw,
    load_sem,
    small_sem,
    halo_send,
    halo_recv,
    row_send,
    row_recv,
    vec_send,
    vec_recv,
):
    r = lax.axis_index("rows")
    v = lax.axis_index("vec")
    bc, bs = self_t.shape[0], self_t.shape[1]
    slots = link_t.shape[1]
    vc, slab = xp.shape[2:]
    kk = vc * n_vec
    nb = links_v.shape[1]
    nc = nb // 2
    lanes = b_gx.shape[2]

    small = [
        pltpu.make_async_copy(vec_hbm, xp.at[v, 0], small_sem.at[0]),
        pltpu.make_async_copy(dir_hbm, xp.at[v, 1], small_sem.at[1]),
        pltpu.make_async_copy(links_hbm, links_s, small_sem.at[2]),
        pltpu.make_async_copy(links_hbm, links_v, small_sem.at[3]),
        pltpu.make_async_copy(coarse_hbm, coarse_s, small_sem.at[4]),
        pltpu.make_async_copy(coarse_hbm, coarse_v, small_sem.at[5]),
    ]
    for load in small:
        load.start()

    def load_block(b):
        return (
            pltpu.make_async_copy(self_hbm.at[b], self_t.at[b], load_sem.at[0, b]),
            pltpu.make_async_copy(link_hbm.at[b], link_t.at[b], load_sem.at[1, b]),
        )

    for b in range(bc):
        for load in load_block(b):
            load.start()

    barrier = pltpu.get_barrier_semaphore()

    def greet_rows(off, c):
        pl.semaphore_signal(
            barrier, inc=1, device_id={"rows": lax.rem(r + off, n_rows)}, device_id_type=MESH
        )
        return c

    def greet_vec(off, c):
        pl.semaphore_signal(
            barrier, inc=1, device_id={"vec": lax.rem(v + off, n_vec)}, device_id_type=MESH
        )
        return c

    lax.fori_loop(1, n_rows, greet_rows, 0, unroll=n_rows <= 16)
    lax.fori_loop(1, n_vec, greet_vec, 0, unroll=n_vec <= 16)

    def over(axis, e, buf, what):
        mine, count = (r, n_rows) if axis == "rows" else (v, n_vec)
        ssem, rsem = (row_send, row_recv) if axis == "rows" else (vec_send, vec_recv)

        def one(off, c):
            other = lax.rem(mine + off, count)
            slot = other if what == "recv" else mine
            copy = pltpu.make_async_remote_copy(
                src_ref=buf.at[slot],
                dst_ref=buf.at[slot],
                send_sem=ssem.at[e, other],
                recv_sem=rsem.at[e, slot],
                device_id={axis: other},
                device_id_type=MESH,
            )
            if what == "start":
                copy.start()
            elif what == "recv":
                copy.wait_recv()
            else:
                copy.wait_send()
            return c

        lax.fori_loop(1, count, one, 0, unroll=count <= 16)

    def halo(e, win, what):
        def copy(direction):
            return pltpu.make_async_remote_copy(
                src_ref=win.at[pl.ds(bc, bc)],
                dst_ref=win.at[pl.ds(0 if direction == 0 else 2 * bc, bc)],
                send_sem=halo_send.at[e, direction],
                recv_sem=halo_recv.at[e, direction],
                device_id={
                    "rows": lax.rem(r + (1 if direction == 0 else n_rows - 1), n_rows)
                },
                device_id_type=MESH,
            )

        has_next = r < n_rows - 1
        has_prev = r > 0
        for direction in range(2):
            sends = has_next if direction == 0 else has_prev
            gets = has_prev if direction == 0 else has_next
            if what == "start":
                pl.when(sends)(lambda d=direction: copy(d).start())
            elif what == "recv":
                pl.when(gets)(lambda d=direction: copy(d).wait_recv())
            else:
                pl.when(sends)(lambda d=direction: copy(d).wait_send())

    def blocks(body):
        def step(b, c):
            body(b, pl.ds(pl.multiple_of(b * bs, bs), bs))
            return c

        lax.fori_loop(0, bc, step, 0, unroll=True)

    base = r * bc
    tiles = (slots + 1) * bc
    total = jnp.zeros((bs, tiles), F32)
    tile_row = iota((tiles, bs), 0)
    for b in range(bc):
        for load in load_block(b):
            load.wait()
        for s in range(slots + 1):
            tile = self_t[b] if s == 0 else link_t[b, s - 1]
            one = jnp.where(tile_row == s * bc + b, 1.0, 0.0).astype(jnp.bfloat16)
            total = total + tile_dot(tile, one)
    rs[...] = total.T
    degree = rs[0:bc]
    for s in range(1, slots + 1):
        degree = degree + rs[s * bc : (s + 1) * bc]
    small[0].wait()
    small[1].wait()
    root = jnp.sqrt(degree)
    inv_root = 1.0 / root
    for b in range(bc):
        at = slice(b * bs, (b + 1) * bs)
        inv = jnp.broadcast_to(inv_root[b : b + 1], (8, bs))
        deg[:, at] = jnp.broadcast_to(root[b : b + 1], (8, bs))
        isq[:, at] = inv
        win1[bc + b, 0:vc] = xp[v, 0, :, at] * inv[0:vc]
        win1[bc + b, vc : 2 * vc] = xp[v, 1, :, at] * inv[0:vc]

    pl.semaphore_wait(barrier, n_rows + n_vec - 2)
    halo(0, win1, "start")
    over("vec", EX_XP, xp, "start")

    lane8 = iota((bc, lanes), 1)
    tile_sums = jnp.zeros((bc, lanes), F32)
    block_degree = jnp.zeros((bc, 1), F32)
    for s in range(slots + 1):
        part = jnp.sum(rs[s * bc : (s + 1) * bc], axis=1, keepdims=True)
        block_degree = block_degree + part
        tile_sums = jnp.where(lane8 == s, part, tile_sums)
    tile_sums = jnp.where(lane8 == slots + 1, block_degree, tile_sums)
    b_gx[r, pl.ds(kk, bc), :] = tile_sums

    def self_part(win):
        total = jnp.zeros((bs, 8 * bc), F32)
        for b in range(bc):
            total = total + tile_dot(self_t[b], in_slot(win[bc + b], b, bc))
        return total

    def links_part(win, total):
        for b in range(bc):
            for s in range(slots):
                place = links_s[s, base + b] - base + bc
                remote = win[jnp.minimum(jnp.maximum(place, 0), 3 * bc - 1)]
                total = total + tile_dot(link_t[b, s], in_slot(remote, b, bc))
        return total.T

    image1 = self_part(win1)

    def diagonal_block(b, at):
        half = 128
        eye = iota((half, half), 0) == iota((half, half), 1)
        parts = []
        for h in range(bs // half):
            cut = self_t[b, h * half : (h + 1) * half, h * half : (h + 1) * half].astype(F32)
            parts.append(jnp.sum(jnp.where(eye, cut, 0.0), axis=0, keepdims=True))
        diag = jnp.concatenate(parts, axis=1)
        inv = isq[:, at]
        dsh[:, at] = damping / (1.0 + spectral_shift - diag * inv * inv)

    blocks(diagonal_block)

    for load in small[2:]:
        load.wait()
    lane_nc = iota((1, nc), 1)
    for s in range(slots + 1):
        for b in range(bc):
            target = base + b if s == 0 else links_s[s - 1, base + b]
            oht[s * bc + b : s * bc + b + 1, :] = (lane_nc == coarse_s[0, target]).astype(F32)

    over("vec", EX_XP, xp, "recv")
    for j in range(n_vec):
        basis[j * vc : (j + 1) * vc, :] = xp[j, 0]
        basis[2 * kk + j * vc : 2 * kk + (j + 1) * vc, :] = xp[j, 1]
    x_all = basis[0:kk, :]
    b_gx[r, 0:kk, 0:kk] = dot_nt(x_all, x_all)
    over("rows", EX_GRAM_X, b_gx, "start")

    halo(0, win1, "recv")
    image1 = links_part(win1, image1)
    for b in range(bc):
        at = slice(b * bs, (b + 1) * bs)
        adj = image1[8 * b : 8 * b + 8] * isq[:, at]
        img[0:vc, at] = xp[v, 0, :, at] - adj[0:vc]
        img[vc : 2 * vc, at] = xp[v, 1, :, at] - adj[vc : 2 * vc]
    b_cross[r, 0:vc, 0:kk] = dot_nt(img[0:vc, :], basis[0:kk, :])
    over("rows", EX_CROSS, b_cross, "start")

    over("rows", EX_GRAM_X, b_gx, "recv")
    got = jnp.sum(b_gx[:, 0:kk, 0:kk], axis=0)
    gram_inv = inverse(got)

    pick_sums = (iota((8, lanes), 0) == iota((8, lanes), 1)).astype(F32)
    sums = b_gx[:, kk : kk + bc, :].reshape(nb, lanes)
    sums_t = dot_nt(pick_sums, sums)
    sub_b, lane_b = iota((nb, nb), 0), iota((nb, nb), 1)
    by_block = jnp.where(sub_b == lane_b, sums_t[0:1], 0.0)
    for s in range(slots):
        by_block = by_block + jnp.where(links_v[s : s + 1] == sub_b, sums_t[s + 1 : s + 2], 0.0)
    pick = (iota((nc, nb), 0) == coarse_v[...]).astype(F32)
    tile_sum = dot_nt(dot_nt(pick, by_block), pick)
    agg = jnp.sum(pick * sums_t[slots + 1 : slots + 2], axis=1, keepdims=True)
    eye_c = iota((nc, nc), 0) == iota((nc, nc), 1)
    coarse = jnp.where(eye_c, (1.0 + spectral_shift) * agg, 0.0) - tile_sum
    to_gain = dot_nt(inverse(coarse), oht[...])

    over("rows", EX_CROSS, b_cross, "recv")
    cross_t = jnp.sum(b_cross[:, :, 0:kk], axis=0)
    coef_t = dot_nn(cross_t, gram_inv)
    residual = img[0:vc, :] - dot_nn(coef_t, basis[0:kk, :])[0:vc]
    res_ref[...] = residual
    out_res = pltpu.make_async_copy(res_ref, res_hbm, small_sem.at[6])
    out_res.start()
    first = residual * dsh[0:vc, :]
    first_r[...] = first

    def put2(b, at):
        win2[bc + b] = first_r[:, at] * isq[0:vc, at]

    blocks(put2)
    halo(1, win2, "start")

    rhs = jnp.zeros((vc, nc), F32)
    direct = (res_ref[...] - (1.0 + spectral_shift) * first) * deg[0:vc, :]
    for b in range(bc):
        sent = win2[bc + b].astype(jnp.bfloat16).astype(F32)
        for s in range(slots + 1):
            t = s * bc + b
            terms = sent * rs[t : t + 1]
            if s == 0:
                terms = terms + direct[:, b * bs : (b + 1) * bs]
            rhs = rhs + jnp.sum(terms, axis=1, keepdims=True) * oht[t : t + 1, :]
    b_rhs[r, 0:vc, 0:nc] = rhs
    over("rows", EX_RHS, b_rhs, "start")

    image2 = self_part(win2)

    halo(1, win2, "recv")
    image2 = links_part(win2, image2)
    for b in range(bc):
        imw[:, b * bs : (b + 1) * bs] = image2[8 * b : 8 * b + vc]
    first = first_r[...]
    r_one = res_ref[...] - (1.0 + spectral_shift) * first + imw[...] * isq[0:vc, :]
    rone_r[...] = r_one
    over("rows", EX_RHS, b_rhs, "recv")
    gain = dot_nn(jnp.sum(b_rhs[:, :, 0:nc], axis=0), to_gain)[0:vc]

    def lift(b, at):
        moved = jnp.zeros((vc, bs), F32)
        for s in range(slots + 1):
            moved = moved + gain_at(s, b) * rs[s * bc + b : s * bc + b + 1]
        inv = isq[0:vc, at]
        lifted = deg[0:vc, at] * gain_at(0, b)
        rest = rone_r[:, at] - (1.0 + spectral_shift) * lifted + moved * inv
        out = first_r[:, at] + lifted + rest * dsh[0:vc, at]
        cor_ref[:, at] = out
        win3[bc + b] = out * inv

    def gain_at(s, b):
        return gain[:, s * bc + b : s * bc + b + 1]

    for b in range(bc):
        lift(b, pl.ds(b * bs, bs))
    halo(2, win3, "start")
    out_cor = pltpu.make_async_copy(cor_ref, cor_hbm, small_sem.at[7])
    out_cor.start()
    wall[v] = cor_ref[...]
    over("vec", EX_W, wall, "start")

    image3 = self_part(win3)

    over("vec", EX_W, wall, "recv")
    for j in range(n_vec):
        basis[kk + j * vc : kk + (j + 1) * vc, :] = wall[j]
    b_gb[r, :, 0 : 3 * kk] = dot_nt(basis[...], basis[...])
    over("rows", EX_GRAM_B, b_gb, "start")

    b_ga[r, 0 : 2 * vc, 0 : 3 * kk] = dot_nt(img[...], basis[...])
    halo(2, win3, "recv")
    image3 = links_part(win3, image3)
    for b in range(bc):
        imw[:, b * bs : (b + 1) * bs] = image3[8 * b : 8 * b + vc]
    imw[...] = cor_ref[...] - imw[...] * isq[0:vc, :]
    b_ga[r, 2 * vc : 3 * vc, 0 : 3 * kk] = dot_nt(imw[...], basis[...])
    over("rows", EX_GRAM_A, b_ga, "start")

    over("rows", EX_GRAM_B, b_gb, "recv")
    linv = inverse_factor(jnp.sum(b_gb[:, :, 0 : 3 * kk], axis=0))

    over("rows", EX_GRAM_A, b_ga, "recv")
    gram_a_t = jnp.sum(b_ga[:, :, 0 : 3 * kk], axis=0)
    fin[v, :, 0 : 3 * kk] = dot_nt(gram_a_t, linv)
    over("vec", EX_FINAL, fin, "start")
    over("vec", EX_FINAL, fin, "recv")
    parts = (
        [fin[j, 0:vc, 0 : 3 * kk] for j in range(n_vec)]
        + [fin[j, 2 * vc : 3 * vc, 0 : 3 * kk] for j in range(n_vec)]
        + [fin[j, vc : 2 * vc, 0 : 3 * kk] for j in range(n_vec)]
    )
    for j, part in enumerate(parts):
        basis[j * vc : (j + 1) * vc, 0 : 3 * kk] = part
    reduced = dot_nn(linv, basis[:, 0 : 3 * kk])
    proj_ref[...] = 0.5 * (reduced + reduced.T)
    out_proj = pltpu.make_async_copy(proj_ref, proj_hbm, small_sem.at[8])
    out_proj.start()

    over("vec", EX_XP, xp, "sent")
    over("vec", EX_W, wall, "sent")
    over("vec", EX_FINAL, fin, "sent")
    over("rows", EX_GRAM_X, b_gx, "sent")
    over("rows", EX_CROSS, b_cross, "sent")
    over("rows", EX_RHS, b_rhs, "sent")
    over("rows", EX_GRAM_B, b_gb, "sent")
    over("rows", EX_GRAM_A, b_ga, "sent")
    halo(0, win1, "sent")
    halo(1, win2, "sent")
    halo(2, win3, "sent")
    out_res.wait()
    out_cor.wait()
    out_proj.wait()


def body(n_rows, n_vec, self_tiles, link_tiles, links, coarse_row, vectors, directions):
    bc, bs = self_tiles.shape[:2]
    slots = link_tiles.shape[1]
    vc, slab = vectors.shape
    nb = links.shape[0]
    nc = nb // 2
    kk = vc * n_vec

    def up(x, m):
        return -(-x // m) * m

    lanes = 128
    basis_lanes = up(3 * kk, 128)
    hbm = pl.BlockSpec(memory_space=pltpu.HBM)
    scratch = [
        pltpu.VMEM((vc, slab), F32),
        pltpu.VMEM((vc, slab), F32),
        pltpu.VMEM((3 * kk, 3 * kk), F32),
        pltpu.SMEM((slots, nb), jnp.int32),
        pltpu.SMEM((1, nb), jnp.int32),
        pltpu.VMEM((slots, nb), jnp.int32),
        pltpu.VMEM((1, nb), jnp.int32),
        pltpu.VMEM((bc, bs, bs), jnp.bfloat16),
        pltpu.VMEM((bc, slots, bs, bs), jnp.bfloat16),
        pltpu.VMEM((n_vec, 2, vc, slab), F32),
        pltpu.VMEM((n_vec, vc, slab), F32),
        pltpu.VMEM((n_vec, up(3 * vc, 8), basis_lanes), F32),
        pltpu.VMEM((3 * bc, 2 * vc, bs), F32),
        pltpu.VMEM((3 * bc, vc, bs), F32),
        pltpu.VMEM((3 * bc, vc, bs), F32),
        pltpu.VMEM((n_rows, kk + bc, lanes), F32),
        pltpu.VMEM((n_rows, up(vc, 8), up(kk, 128)), F32),
        pltpu.VMEM((n_rows, up(vc, 8), up(nc, 128)), F32),
        pltpu.VMEM((n_rows, 3 * kk, basis_lanes), F32),
        pltpu.VMEM((n_rows, up(3 * vc, 8), basis_lanes), F32),
        pltpu.VMEM((3 * kk, slab), F32),
        pltpu.VMEM((8, slab), F32),
        pltpu.VMEM((8, slab), F32),
        pltpu.VMEM((8, slab), F32),
        pltpu.VMEM(((slots + 1) * bc, bs), F32),
        pltpu.VMEM((2 * vc, slab), F32),
        pltpu.VMEM(((slots + 1) * bc, nc), F32),
        pltpu.VMEM((vc, slab), F32),
        pltpu.VMEM((vc, slab), F32),
        pltpu.VMEM((vc, slab), F32),
        pltpu.SemaphoreType.DMA((2, bc)),
        pltpu.SemaphoreType.DMA((9,)),
        pltpu.SemaphoreType.DMA((3, 2)),
        pltpu.SemaphoreType.DMA((3, 2)),
        pltpu.SemaphoreType.DMA((5, n_rows)),
        pltpu.SemaphoreType.DMA((5, n_rows)),
        pltpu.SemaphoreType.DMA((3, n_vec)),
        pltpu.SemaphoreType.DMA((3, n_vec)),
    ]
    out_shape = (
        jax.ShapeDtypeStruct((vc, slab), F32),
        jax.ShapeDtypeStruct((vc, slab), F32),
        jax.ShapeDtypeStruct((3 * kk, 3 * kk), F32),
    )
    results = pl.pallas_call(
        functools.partial(kernel, n_rows, n_vec),
        out_shape=out_shape,
        in_specs=[hbm] * 6,
        out_specs=(hbm, hbm, hbm),
        scratch_shapes=scratch,
        compiler_params=pltpu.CompilerParams(
            collective_id=0, has_side_effects=True, vmem_limit_bytes=63 * 1024 * 1024
        ),
    )(
        self_tiles,
        link_tiles,
        links.T,
        coarse_row.reshape(1, nb),
        vectors,
        directions,
    )
    return pl.pallas_call(
        hand_over,
        out_shape=out_shape,
        in_specs=[hbm] * 3,
        out_specs=(hbm, hbm, hbm),
        scratch_shapes=[pltpu.VMEM(o.shape, F32) for o in out_shape]
        + [pltpu.SemaphoreType.DMA((2, 3))],
        compiler_params=pltpu.CompilerParams(vmem_limit_bytes=63 * 1024 * 1024),
    )(*results)


def hand_over(a, b, c, out_a, out_b, out_c, held_a, held_b, held_c, sem):
    refs = ((a, held_a, out_a), (b, held_b, out_b), (c, held_c, out_c))
    gets = [pltpu.make_async_copy(x, h, sem.at[0, i]) for i, (x, h, _) in enumerate(refs)]
    puts = [pltpu.make_async_copy(h, y, sem.at[1, i]) for i, (_, h, y) in enumerate(refs)]
    for copy in gets:
        copy.start()
    for get, put in zip(gets, puts):
        get.wait()
        put.start()
    for copy in puts:
        copy.wait()


def solution(mesh):
    in_specs = (
        P("rows", None, None),
        P("rows", None, None, None),
        P(),
        P(),
        P("vec", "rows"),
        P("vec", "rows"),
    )
    out_specs = (P("vec", "rows"), P("vec", "rows"), P())
    return jax.shard_map(
        functools.partial(body, mesh.shape["rows"], mesh.shape["vec"]),
        mesh=mesh,
        in_specs=in_specs,
        out_specs=out_specs,
        check_vma=False,
    )
```
